128 devices in a mesh: tensor: 4 (over z_lo, core), expert: 32 (over y, x, z_hi).
Axes of the slice: x: 4, y: 4, z: 4 (z_hi: 2, z_lo: 2; z = z_hi * 2 + z_lo), core: 2. Of those that a mesh axis runs over, the one named last changes fastest.
Arguments:
- gate_weights: bfloat16 [32, 7168, 2048], P(None, 'expert', 'tensor'), may hold values from -0.0625 to 0.0625
- test_blocks: bfloat16 [32, 2048, 512], P('expert', 'tensor'), may hold values from -6 to 6
Outputs:
- basis: float32 [7168, 512], P('expert')
- coefficients: bfloat16 [32, 512, 2048], P('expert', None, 'tensor')
The draws below stay inside these ranges and needn't reach their ends.
All inputs are finite; a program needn't handle non-finite values.
Results may differ from the reference program's by a relative error of at most 0.0047.
Values may be sent and summed in bfloat16 or wider, within the bound.
A program may use at most 128 MiB of HBM per device.

```python
import jax
import jax.numpy as jnp
from jax import lax

D = 7168
FF = 2048
K = 512
EXPERTS = 32


def levels(key, extent, pieces, smallest, top_value):
    loudness, own = 1.0, jax.random.fold_in(key, 6)
    for dim, blocks in pieces:
        heights = jnp.exp(jax.random.uniform(jax.random.fold_in(own, dim), (blocks,), jnp.float32, smallest / len(pieces), top_value / len(pieces)))
        loudness = loudness * jnp.repeat(heights, extent[dim] // blocks).reshape([-1 if axis == dim else 1 for axis in range(len(extent))])
    return loudness


def centred(stream_key, extent, spread, most, shards=(), held_as=jnp.bfloat16):
    gain = levels(stream_key, extent, shards, -0.22, 0.18) if shards else 1.0
    drawn = jax.random.normal(stream_key, extent, jnp.float32) * spread * gain
    return jnp.minimum(jnp.maximum(drawn, -most), most).astype(held_as)


def setup_inputs(seed: int = 0) -> dict:
    keys = jax.random.split(jax.random.key(seed), 3)
    return {
        "gate_weights": centred(keys[0], (EXPERTS, D, FF), D ** -0.5, 0.0625, ((1, 32), (2, 4))),
        "test_blocks": centred(keys[1], (EXPERTS, FF, K), 1.0, 6.0, ((0, 32), (1, 4))),
    }


def reference(gate_weights, test_blocks):

    def add_expert(total, pair):
        weight, block = pair
        return (total + jnp.dot(weight.astype(jnp.float32), block.astype(jnp.float32), preferred_element_type=jnp.float32), None)
    start = jnp.zeros((D, K), jnp.float32)
    sketch, unused = lax.scan(add_expert, start, (gate_weights, test_blocks))
    gram = jnp.dot(sketch.T, sketch, precision=lax.Precision.HIGHEST) / D
    lower = jnp.linalg.cholesky(gram)
    basis = lax.linalg.triangular_solve(lower, sketch, left_side=False, lower=True, transpose_a=True)
    basis_half = basis.astype(jnp.bfloat16)

    def project(weight):
        return jnp.dot(basis_half.T.astype(jnp.float32), weight.astype(jnp.float32), preferred_element_type=jnp.float32).astype(jnp.bfloat16)
    coefficients = lax.map(project, gate_weights)
    return (basis, coefficients)
```

```python
import functools

import jax
import jax.numpy as jnp
from jax import lax
from jax.experimental import pallas as pl
from jax.experimental.pallas import tpu as pltpu
from jax.sharding import PartitionSpec as P

MESH = pl.DeviceIdType.MESH
F32, BF16 = jnp.float32, jnp.bfloat16
SIDE = 4
CHIP_ROWS = 112
HALF = 256
GROUPS = ((0, 48, "xyz"), (48, 32, "yzx"), (80, 32, "zxy"))


def where():
    t, e = lax.axis_index("tensor"), lax.axis_index("expert")
    return {"y": e // 8, "x": (e // 2) % 4, "z": (e % 2) * 2 + t // 2, "c": t % 2}


def device(at):
    return (at["z"] % 2) * 2 + at["c"], (at["y"] * 4 + at["x"]) * 2 + at["z"] // 2


def moved(at, axis, by):
    return {**at, axis: lax.rem(at[axis] + by, 2 if axis == "c" else SIDE)}


def send(src, dst, sems, index, at):
    copy = pltpu.make_async_remote_copy(
        src_ref=src, dst_ref=dst, send_sem=sems[0].at[index], recv_sem=sems[1].at[index],
        device_id=device(at), device_id_type=MESH,
    )
    copy.start()
    return copy


def cut(ref, dims, fixed, rows, lead=()):
    return ref.at[(*lead, *(fixed.get(d, slice(None)) for d in dims), rows)]


def sum_kernel(g_hbm, t_ref, f_ref, g, away, landed, q, *rest):
    stage1, sums1, stage2, sums2, stage3 = (rest[3 * i:3 * i + 3] for i in range(5))
    load_sem, *sems = rest[15:]
    core_sems, rs_sems, ag_sems, pair_sems = (sems[2 * i:2 * i + 2] for i in range(4))
    me = where()
    c = me["c"]
    loads = []
    for y in range(SIDE):
        load = pltpu.make_async_copy(g_hbm.at[pl.ds(y * 1792, 1792)], g.at[pl.ds(y * 1792, 1792)], load_sem.at[y])
        load.start()
        loads.append(load)

    peers = [moved(me, "c", 1)] + [moved(me, a, k) for a in "xyz" for k in (1, 2, 3)]
    barrier = pltpu.get_barrier_semaphore()
    for peer in peers:
        pl.semaphore_signal(barrier, inc=1, device_id=device(peer), device_id_type=MESH)
    pl.semaphore_wait(barrier, len(peers))

    def product(y, x, column):
        start = pl.multiple_of((y * SIDE + x) * 448, 448)
        return jnp.dot(
            g[pl.ds(start, 448)], t_ref[:, pl.ds(pl.multiple_of(column * HALF, HALF), HALF)],
            preferred_element_type=F32,
        )

    pairs = []
    for y in range(SIDE):
        loads[y].wait()

        @pl.loop(0, SIDE)
        def _(x):
            away[y, x] = product(y, x, 1 - c).astype(BF16).reshape(SIDE, CHIP_ROWS, HALF)

        pairs.append(send(away.at[y], landed.at[y], core_sems, y, peers[0]))
    for y in range(SIDE):
        pairs[y].wait_recv()

        @pl.loop(0, SIDE)
        def _(x):
            own = product(y, x, c).reshape(SIDE, CHIP_ROWS, HALF)
            q[y, x] = (own + landed[y, x].astype(F32)).astype(BF16)

    copies = []

    def exchange(step, source, dims, slots, rows_of):
        started = []
        for i, (first, rows, order) in enumerate(GROUPS):
            axis = order[step]
            for k in (1, 2, 3):
                peer = moved(me, axis, k)
                started.append(send(
                    cut(source(i), dims(order), {axis: peer[axis]}, rows_of(first, rows)),
                    slots[i].at[k - 1], rs_sems, step * 9 + i * 3 + k - 1, peer,
                ))
        copies.extend(started)
        return started

    def add(step, source, dims, slots, totals, rows_of):
        for i, (first, rows, order) in enumerate(GROUPS):
            axis = order[step]
            for k in range(3):
                started[i * 3 + k].wait_recv()
            mine = cut(source(i), dims(order), {axis: me[axis]}, rows_of(first, rows))
            lead = slots[i].shape[1:-2]

            def one(at):
                total = mine[(*at,)].astype(F32)
                for k in range(3):
                    total += slots[i][(k, *at)].astype(F32)
                totals[i][(*at,)] = total

            if len(lead) == 2:
                @pl.loop(0, SIDE)
                def _(a):
                    for b in range(SIDE):
                        one((a, b))
            else:
                for a in range(SIDE):
                    one((a,))

    def remaining(step):
        return lambda order: "".join(d for d in "yxz" if d not in order[:step])

    group_rows = lambda first, rows: pl.ds(first, rows)
    all_rows = lambda first, rows: slice(None)
    started = exchange(0, lambda i: q, remaining(0), stage1, group_rows)
    add(0, lambda i: q, remaining(0), stage1, sums1, group_rows)
    started = exchange(1, lambda i: sums1[i], remaining(1), stage2, all_rows)
    add(1, lambda i: sums1[i], remaining(1), stage2, sums2, all_rows)
    started = exchange(2, lambda i: sums2[i], remaining(2), stage3, all_rows)
    for i, (first, rows, order) in enumerate(GROUPS):
        axis = order[2]
        total = sums2[i][me[axis]]
        for k in range(3):
            started[i * 3 + k].wait_recv()
            total += stage3[i][k]
        f_ref[c, me["y"], me["x"], me["z"], pl.ds(first, rows)] = total.astype(BF16)

    twin, shared = peers[0], []

    def share(i, fixed, index):
        first, rows, _ = GROUPS[i]
        part = cut(f_ref, "yxz", fixed, pl.ds(first, rows), (c,))
        shared.append(send(part, part, pair_sems, index, twin))

    for step in (2, 1, 0):
        started = []
        for i, (first, rows, order) in enumerate(GROUPS):
            axis = order[step]
            fixed = {a: me[a] for a in order[:step + 1]}
            part = cut(f_ref, "yxz", fixed, pl.ds(first, rows), (c,))
            for k in (1, 2, 3):
                started.append(send(part, part, ag_sems, step * 9 + i * 3 + k - 1, moved(me, axis, k)))
            if step == 0:
                share(i, fixed, i * 4)
        for i, (first, rows, order) in enumerate(GROUPS):
            axis = order[step]
            for k in (1, 2, 3):
                started[i * 3 + k - 1].wait_recv()
                if step == 0:
                    share(i, {axis: lax.rem(me[axis] + SIDE - k, SIDE)}, i * 4 + k)
        copies.extend(started)
    for copy in copies + pairs + shared:
        copy.wait_send()
    for copy in shared:
        copy.wait_recv()


def finish_kernel(f_ref, g_ref, f_any, basis_ref, c_ref, ok_ref, acc, own, sem):
    step = pl.program_id(0)
    e = lax.axis_index("expert")

    @pl.when(step == 0)
    def _():
        acc[...] = jnp.zeros_like(acc)
        pltpu.make_async_copy(f_any.at[:, pl.ds(pl.multiple_of(e * 224, 224), 224)], own, sem).start()

    s = jnp.concatenate([f_ref[0], f_ref[1]], axis=1)
    acc[...] += lax.dot_general(
        s, jnp.concatenate([s, g_ref[...]], axis=1), (((0,), (0,)), ((), ())), preferred_element_type=F32
    )

    @pl.when(step == pl.num_programs(0) - 1)
    def _():
        pltpu.make_async_copy(f_any.at[:, pl.ds(pl.multiple_of(e * 224, 224), 224)], own, sem).wait()
        k = acc.shape[0]
        row = lax.broadcasted_iota(jnp.int32, (k, k), 0)
        col = lax.broadcasted_iota(jnp.int32, (k, k), 1)
        eye = (row == col).astype(F32)
        gram = acc[:, :k] / 7168
        diagonal = gram * eye
        down = lax.rsqrt(jnp.sum(diagonal, axis=1, keepdims=True))
        across = lax.rsqrt(jnp.sum(diagonal, axis=0, keepdims=True))
        a = gram * down * across

        def dot(u, v, across=False):
            return lax.dot_general(u, v, (((1,), (1 if across else 0,)), ((), ())), preferred_element_type=F32)

        def halves(u):
            high = u.astype(BF16)
            return high, (u - high.astype(F32)).astype(BF16)

        def fine(u, v, across=False):
            (uh, ul), (vh, vl) = halves(u), halves(v)
            return dot(uh, vh, across) + (dot(uh, vl, across) + dot(ul, vh, across))

        def coarse(u, v, across=False):
            return dot(u.astype(BF16), v.astype(BF16), across)

        half_lower = jnp.where(row > col, 1.0, 0.5 * eye)

        def gap(x, mul):
            return mul(mul(x, a), x, True) - eye

        def better(x, e, mul):
            phi = e * half_lower
            y = mul(phi, x)
            return x - (y - mul(phi, y))

        phi = (a - eye) * half_lower
        x = eye - (phi - coarse(phi, phi))
        x = better(x, gap(x, coarse), coarse)
        x = better(x, gap(x, fine), fine)
        left = gap(x, fine)
        ok_ref[0, 0] = jnp.sum(left * left)
        x = x * across
        c_ref[...] = fine(x, acc[:, k:]).astype(BF16)
        high, low = halves(x)
        rows = jnp.concatenate([own[0], own[1]], axis=1)
        basis_ref[...] = dot(rows, high, True) + dot(rows, low, True)


def local(gate_weights, test_blocks):
    owned = lax.all_to_all(gate_weights, "expert", split_axis=0, concat_axis=1, tiled=True)[0]
    block = test_blocks[0]
    shape = lambda step, order, rows: tuple(SIDE for _ in range(3 - step)) + (rows, HALF)
    scratch = [
        pltpu.VMEM((7168, 512), BF16),
        pltpu.VMEM((SIDE, SIDE, SIDE, CHIP_ROWS, HALF), BF16),
        pltpu.VMEM((SIDE, SIDE, SIDE, CHIP_ROWS, HALF), BF16),
        pltpu.VMEM((SIDE, SIDE, SIDE, CHIP_ROWS, HALF), BF16),
    ]
    for step, kind in ((1, BF16), (2, F32), (3, F32)):
        scratch += [pltpu.VMEM((3,) + shape(step, order, rows), kind) for _, rows, order in GROUPS]
        if step < 3:
            scratch += [pltpu.VMEM(shape(step, order, rows), F32) for _, rows, order in GROUPS]
    scratch += [pltpu.SemaphoreType.DMA((4,))]
    for count in (4, 27, 27, 12):
        scratch += [pltpu.SemaphoreType.DMA((count,))] * 2
    whole = pl.pallas_call(
        sum_kernel,
        out_shape=jax.ShapeDtypeStruct((2, SIDE, SIDE, SIDE, CHIP_ROWS, HALF), BF16),
        in_specs=[pl.BlockSpec(memory_space=pl.ANY), pl.BlockSpec(memory_space=pltpu.VMEM)],
        out_specs=pl.BlockSpec(memory_space=pltpu.VMEM),
        scratch_shapes=scratch,
        compiler_params=pltpu.CompilerParams(collective_id=0, has_side_effects=True, vmem_limit_bytes=56 << 20),
    )(owned, block)
    whole = whole.reshape(2, 7168, HALF)
    steps = 8
    deep = 7168 // steps
    basis, coefficients, gap = pl.pallas_call(
        finish_kernel,
        grid=(steps,),
        out_shape=(
            jax.ShapeDtypeStruct((224, 512), F32),
            jax.ShapeDtypeStruct((512, 512), BF16),
            jax.ShapeDtypeStruct((1, 1), F32),
        ),
        in_specs=[
            pl.BlockSpec((2, deep, HALF), lambda i: (0, i, 0)),
            pl.BlockSpec((deep, 512), lambda i: (i, 0)),
            pl.BlockSpec(memory_space=pl.ANY),
        ],
        out_specs=(
            pl.BlockSpec((224, 512), lambda i: (0, 0)),
            pl.BlockSpec((512, 512), lambda i: (0, 0)),
            pl.BlockSpec(memory_space=pltpu.SMEM),
        ),
        scratch_shapes=[
            pltpu.VMEM((512, 1024), F32), pltpu.VMEM((2, 224, HALF), BF16), pltpu.SemaphoreType.DMA(()),
        ],
        compiler_params=pltpu.CompilerParams(vmem_limit_bytes=56 << 20),
    )(whole, owned, whole)

    def exact():
        s = jnp.concatenate([whole[0], whole[1]], axis=1)
        dots = functools.partial(jnp.einsum, preferred_element_type=F32)
        lower = jnp.linalg.cholesky(dots("rk,rl->kl", s, s) / 7168)
        x = lax.linalg.triangular_solve(lower, jnp.eye(512, dtype=F32), left_side=True, lower=True)
        rows = lax.dynamic_slice_in_dim(s, lax.axis_index("expert") * 224, 224, 0)
        high = functools.partial(jnp.dot, precision=lax.Precision.HIGHEST)
        return high(rows.astype(F32), x.T), high(x, dots("rk,rf->kf", s, owned)).astype(BF16)

    basis, coefficients = lax.cond(gap[0, 0] < 1e-4, lambda: (basis, coefficients), exact)
    return basis, coefficients[None]


def solution(mesh):
    placed = (P(None, "expert", "tensor"), P("expert", "tensor", None))
    return jax.shard_map(
        local,
        mesh=mesh,
        in_specs=placed,
        out_specs=(P("expert", None), P("expert", None, "tensor")),
        check_vma=False,
    )
```

```python
import functools

import jax
import jax.numpy as jnp
from jax import lax
from jax.experimental import pallas as pl
from jax.experimental.pallas import tpu as pltpu
from jax.sharding import PartitionSpec as P

MESH = pl.DeviceIdType.MESH
F32, BF16 = jnp.float32, jnp.bfloat16
SIDE = 4
CHIP_ROWS = 112
HALF = 256
PARTS = ((0, 32, "xyz"), (32, 16, "yzx"), (48, 16, "zxy"), (64, 16, "xyz"), (80, 16, "yzx"), (96, 16, "zxy"))
BATCHES = ((1, 2, 0), (4, 5, 3))
ALL = sum(BATCHES, ())


def where():
    t, e = lax.axis_index("tensor"), lax.axis_index("expert")
    return {"y": e // 8, "x": (e // 2) % 4, "z": (e % 2) * 2 + t // 2, "c": t % 2}


def device(at):
    return (at["z"] % 2) * 2 + at["c"], (at["y"] * 4 + at["x"]) * 2 + at["z"] // 2


def moved(at, axis, by):
    return {**at, axis: lax.rem(at[axis] + by, 2 if axis == "c" else SIDE)}


def send(src, dst, sems, index, at):
    copy = pltpu.make_async_remote_copy(
        src_ref=src, dst_ref=dst, send_sem=sems[0].at[index], recv_sem=sems[1].at[index],
        device_id=device(at), device_id_type=MESH,
    )
    copy.start()
    return copy


def cut(ref, fixed, rows=None, lead=(), dims="yxz", extra=()):
    tail = () if rows is None else (*extra, rows)
    return ref.at[(*lead, *(fixed.get(d, slice(None)) for d in dims), *tail)]


def sum_kernel(g_hbm, t_ref, acc, own_rows, *rest):
    count = len(PARTS)

    def take(n):
        nonlocal rest
        taken, rest = rest[:n], rest[n:]
        return taken

    g, f_ref = take(2)
    turned1, turned2 = take(count), take(count)
    away, landed, q = take(count), take(count), take(count)
    stage1, sums1, stage2, sums2, stage3 = (take(count) for _ in range(5))
    (local_sem,) = take(1)
    turn_sems, core_sems, rs_sems, ag_sems, pair_sems = (take(2) for _ in range(5))
    me = where()
    c = me["c"]
    twin = moved(me, "c", 1)
    peers = [twin] + [moved(me, a, k) for a in "xyz" for k in (1, 2, 3)]
    barrier = pltpu.get_barrier_semaphore()
    for peer in peers:
        pl.semaphore_signal(barrier, inc=1, device_id=device(peer), device_id_type=MESH)
    pl.semaphore_wait(barrier, len(peers))
    sent = []

    def turn(p, step):
        first, rows, order = PARTS[p]
        axis, at = order[step], pl.ds(first, rows)
        either = (slice(None),)
        place = lambda spot: {axis: spot[axis] // 2 if axis == "z" else spot[axis]}
        source = lambda fixed: cut(g_hbm, fixed, at, extra=either) if step == 0 else cut((turned1, turned2)[step - 1][p], fixed)
        target = lambda fixed: cut(g, fixed, at, extra=either) if step == 2 else cut((turned1, turned2)[step][p], fixed)
        kept = pltpu.make_async_copy(source(place(me)), target(place(me)), local_sem.at[p * 3 + step])
        kept.start()
        started = []
        for k in (2,) if axis == "z" else (2, 1, 3):
            peer = moved(me, axis, k)
            started.append(send(source(place(peer)), target(place(me)), turn_sems, p * 9 + step * 3 + k - 1, peer))
        sent.extend(started)
        return kept, started

    def turned(copies):
        copies[0].wait()
        for copy in copies[1]:
            copy.wait_recv()

    moves = {p: turn(p, 0) for p in ALL}
    for step in (1, 2):
        for p in ALL:
            turned(moves[p])
            moves[p] = turn(p, step)

    def product(p, y, column):
        first, rows, _ = PARTS[p]
        left = g[y, :, :, :, pl.ds(first, rows)].reshape(16 * rows, 512)
        right = t_ref[:, pl.ds(pl.multiple_of(column * HALF, HALF), HALF)]
        return jnp.dot(left, right, preferred_element_type=F32).reshape(SIDE, SIDE, rows, HALF)

    def pair(p):
        @pl.loop(0, SIDE)
        def _(y):
            away[p][y] = product(p, y, 1 - c).astype(BF16)

        copy = send(away[p], landed[p], core_sems, p, twin)
        sent.append(copy)
        return copy

    def both(p, copy):
        copy.wait_recv()

        @pl.loop(0, SIDE)
        def _(y):
            q[p][y] = (product(p, y, c) + landed[p][y].astype(F32)).astype(BF16)

    sources, slots, totals = (q, sums1, sums2), (stage1, stage2, stage3), (sums1, sums2)

    def left_after(p, step):
        return "".join(d for d in "yxz" if d not in PARTS[p][2][:step])

    def scatter(p, step):
        axis, started = PARTS[p][2][step], []
        for k in (2, 1, 3):
            peer = moved(me, axis, k)
            source = cut(sources[step][p], {axis: peer[axis]}, dims=left_after(p, step))
            started.append(send(source, slots[step][p].at[k - 1], rs_sems, p * 9 + step * 3 + k - 1, peer))
        sent.extend(started)
        return started

    def add(p, step, started):
        first, rows, order = PARTS[p]
        axis = order[step]
        for copy in started:
            copy.wait_recv()
        mine = cut(sources[step][p], {axis: me[axis]}, dims=left_after(p, step))

        def total(at):
            value = mine[(*at,)].astype(F32)
            for k in range(3):
                value += slots[step][p][(k, *at)].astype(F32)
            return value

        if step == 0:
            @pl.loop(0, SIDE)
            def _(a):
                totals[0][p][a] = total((a,))
        elif step == 1:
            totals[1][p][...] = total((slice(None),))
        else:
            f_ref[c, me["y"], me["x"], me["z"], pl.ds(first, rows)] = total((slice(None),)).astype(BF16)

    def gather(p, step):
        first, rows, order = PARTS[p]
        part = cut(f_ref, {a: me[a] for a in order[:step + 1]}, pl.ds(first, rows), (c,))
        started = [
            send(part, part, ag_sems, p * 9 + step * 3 + k - 1, moved(me, order[step], k)) for k in (2, 1, 3)
        ]
        sent.extend(started)
        return started

    def share(p, k):
        first, rows, order = PARTS[p]
        axis = order[0]
        part = cut(f_ref, {axis: lax.rem(me[axis] + SIDE - k, SIDE)}, pl.ds(first, rows), (c,))
        copy = send(part, part, pair_sems, p * SIDE + k, twin)
        sent.append(copy)
        return copy

    pairs = {}
    for batch in BATCHES:
        for p in batch:
            turned(moves[p])
            pairs[p] = pair(p)
        for p in batch:
            both(p, pairs[p])
            moves[p] = scatter(p, 0)
    for step in range(3):
        for batch in BATCHES:
            for p in batch:
                add(p, step, moves[p])
                moves[p] = scatter(p, step + 1) if step < 2 else gather(p, 2)
    for step in (1, 0):
        for batch in BATCHES:
            for p in batch:
                for copy in moves[p]:
                    copy.wait_recv()
                moves[p] = gather(p, step)
                if step == 0:
                    pairs[p] = [share(p, 0)]
    for batch in BATCHES:
        for p in batch:
            for copy, k in zip(moves[p], (2, 1, 3)):
                copy.wait_recv()
                pairs[p].append(share(p, k))
    acc[...] = jnp.zeros_like(acc)
    for batch in BATCHES:
        for p in batch:
            for copy in pairs[p]:
                copy.wait_recv()
            first, rows, _ = PARTS[p]

            @pl.loop(0, SIDE)
            def _(y):
                at = pl.ds(first, rows)
                s = jnp.concatenate([f_ref[h, y, :, :, at].reshape(16 * rows, HALF) for h in (0, 1)], axis=1)
                w = g[y, :, :, :, at].reshape(16 * rows, 512)
                acc[...] += lax.dot_general(
                    s, jnp.concatenate([s, w], axis=1), (((0,), (0,)), ((), ())), preferred_element_type=F32
                )

    for h in (0, 1):
        own_rows[h] = f_ref[h, me["y"], me["x"], pl.ds(me["z"] // 2 * 2, 2)]
    for copy in sent:
        copy.wait_send()


def finish_kernel(acc, own, basis_ref, c_ref, ok_ref):
    k = acc.shape[0]
    row = lax.broadcasted_iota(jnp.int32, (k, k), 0)
    col = lax.broadcasted_iota(jnp.int32, (k, k), 1)
    eye = (row == col).astype(F32)
    gram = acc[:, :k] / 7168
    diagonal = gram * eye
    down = lax.rsqrt(jnp.sum(diagonal, axis=1, keepdims=True))
    across = lax.rsqrt(jnp.sum(diagonal, axis=0, keepdims=True))
    a = gram * down * across

    def dot(u, v, across=False):
        return lax.dot_general(u, v, (((1,), (1 if across else 0,)), ((), ())), preferred_element_type=F32)

    def halves(u):
        high = u.astype(BF16)
        return high, (u - high.astype(F32)).astype(BF16)

    def fine(u, v, across=False):
        (uh, ul), (vh, vl) = halves(u), halves(v)
        return dot(uh, vh, across) + (dot(uh, vl, across) + dot(ul, vh, across))

    def coarse(u, v, across=False):
        return dot(u.astype(BF16), v.astype(BF16), across)

    half_lower = jnp.where(row > col, 1.0, 0.5 * eye)

    def gap(x, mul):
        return mul(mul(x, a), x, True) - eye

    def better(x, e, mul):
        phi = e * half_lower
        y = mul(phi, x)
        return x - (y - mul(phi, y))

    phi = (a - eye) * half_lower
    x = eye - (phi - coarse(phi, phi))
    x = better(x, gap(x, coarse), coarse)
    x = better(x, gap(x, fine), fine)
    left = gap(x, fine)
    ok_ref[0, 0] = jnp.sum(left * left)
    x = x * across
    c_ref[...] = fine(x, acc[:, k:]).astype(BF16)
    high, low = halves(x)
    rows = jnp.concatenate([own[0], own[1]], axis=1)
    basis_ref[...] = dot(rows, high, True) + dot(rows, low, True)


def local(gate_weights, test_blocks):
    weights = gate_weights.reshape(SIDE, SIDE, 2, 2, CHIP_ROWS, 512)
    spread = lambda step, rows: tuple(SIDE for _ in range(3 - step)) + (rows, HALF)
    sizes = [rows for _, rows, _ in PARTS]
    scratch = [
        pltpu.VMEM((SIDE, SIDE, 2, 2, CHIP_ROWS, 512), BF16),
        pltpu.VMEM((2, SIDE, SIDE, SIDE, CHIP_ROWS, HALF), BF16),
    ]
    scratch += [pltpu.VMEM((SIDE, SIDE, 2, 2, rows, 512), BF16) for rows in sizes * 2]
    scratch += [pltpu.VMEM(spread(0, rows), BF16) for rows in sizes * 3]
    for step, kind in ((1, BF16), (2, F32), (3, F32)):
        scratch += [pltpu.VMEM((3,) + spread(step, rows), kind) for rows in sizes]
        if step < 3:
            scratch += [pltpu.VMEM(spread(step, rows), F32) for rows in sizes]
    n = len(PARTS)
    scratch += [pltpu.SemaphoreType.DMA((3 * n,))]
    for size in (9, 1, 9, 9, 4):
        scratch += [pltpu.SemaphoreType.DMA((size * n,))] * 2
    vmem, hbm = pl.BlockSpec(memory_space=pltpu.VMEM), pl.BlockSpec(memory_space=pl.ANY)
    acc, rows = pl.pallas_call(
        sum_kernel,
        out_shape=(
            jax.ShapeDtypeStruct((512, 1024), F32),
            jax.ShapeDtypeStruct((2, 2, CHIP_ROWS, HALF), BF16),
        ),
        in_specs=[hbm, vmem],
        out_specs=(vmem, vmem),
        scratch_shapes=scratch,
        compiler_params=pltpu.CompilerParams(collective_id=0, has_side_effects=True, vmem_limit_bytes=60 << 20),
    )(weights, test_blocks[0])
    rows = rows.reshape(2, 224, HALF)
    basis, coefficients, gap = pl.pallas_call(
        finish_kernel,
        out_shape=(
            jax.ShapeDtypeStruct((224, 512), F32),
            jax.ShapeDtypeStruct((512, 512), BF16),
            jax.ShapeDtypeStruct((1, 1), F32),
        ),
        in_specs=[vmem, vmem],
        out_specs=(vmem, vmem, pl.BlockSpec(memory_space=pltpu.SMEM)),
        compiler_params=pltpu.CompilerParams(vmem_limit_bytes=60 << 20),
    )(acc, rows)

    def exact():
        lower = jnp.linalg.cholesky(acc[:, :512] / 7168)
        x = lax.linalg.triangular_solve(lower, jnp.eye(512, dtype=F32), left_side=True, lower=True)
        high = functools.partial(jnp.dot, precision=lax.Precision.HIGHEST)
        s = jnp.concatenate([rows[0], rows[1]], axis=1).astype(F32)
        return high(s, x.T), high(x, acc[:, 512:]).astype(BF16)

    basis, coefficients = lax.cond(gap[0, 0] < 1e-4, lambda: (basis, coefficients), exact)
    return basis, coefficients[None]


def solution(mesh):
    placed = (P(None, "expert", "tensor"), P("expert", "tensor", None))
    return jax.shard_map(
        local,
        mesh=mesh,
        in_specs=placed,
        out_specs=(P("expert", None), P("expert", None, "tensor")),
        check_vma=False,
    )
```

```python
import functools

import jax
import jax.numpy as jnp
from jax import lax
from jax.experimental import pallas as pl
from jax.experimental.pallas import tpu as pltpu
from jax.sharding import PartitionSpec as P

MESH = pl.DeviceIdType.MESH
F32, BF16 = jnp.float32, jnp.bfloat16
SIDE = 4
CHIP_ROWS = 112
HALF = 256
VMEM_LIMIT = 62 << 20
ROWS = 16
ORDERS = ("xyz", "yzx", "zxy", "xyz", "yzx", "zxy", "xyz")
AROUND = (0, 1, 5, 6)
PASSED = (0, 1, 3, 4)
TURN_ORDERS = ("xyz", "yzx", "zxy")
PLAN = (
    ("turn", 0, 0), ("turn", 1, 0), ("turn", 2, 0), ("turn", 3, 0), ("turn", 4, 0), ("turn", 5, 0), ("turn", 6, 0),
    ("turn", 7, 0), ("turn", 8, 0), ("turn", 9, 0), ("turn", 10, 0), ("turn", 11, 0), ("turn", 12, 0),
    ("turn", 13, 0), ("turn", 1, 1), ("turn", 2, 1), ("turn", 0, 1), ("turn", 4, 1), ("turn", 5, 1), ("turn", 3, 1),
    ("turn", 7, 1), ("turn", 8, 1), ("turn", 6, 1), ("turn", 10, 1), ("turn", 11, 1), ("turn", 9, 1), ("turn", 13, 1),
    ("turn", 1, 2), ("turn", 12, 1), ("turn", 0, 2), ("turn", 4, 2), ("turn", 2, 2), ("turn", 3, 2), ("turn", 7, 2),
    ("turn", 5, 2), ("turn", 6, 2), ("turn", 10, 2), ("turn", 8, 2), ("turn", 9, 2), ("turn", 13, 2), ("turn", 11, 2),
    ("pair", 0), ("both", 0), ("turn", 12, 2), ("pair", 1), ("both", 1), ("pair", 2), ("pair", 3), ("both", 2),
    ("both", 3), ("pair", 4), ("both", 4), ("pair", 5), ("pair", 6), ("onward", 0), ("onward", 1), ("both", 5),
    ("both", 6), ("add", 2, 0), ("add", 3, 0), ("add", 4, 0), ("onward", 5), ("add", 0, 0), ("add", 1, 0),
    ("onward", 6), ("add", 4, 1), ("add", 3, 1), ("add", 2, 1), ("add", 5, 0), ("add", 0, 1), ("add", 6, 0),
    ("add", 2, 2), ("add", 4, 2), ("add", 1, 1), ("add", 3, 2), ("add", 0, 2), ("add", 5, 1), ("further", 4, 1),
    ("further", 3, 1), ("add", 1, 2), ("add", 6, 1), ("further", 0, 1), ("further", 2, 1), ("add", 5, 2),
    ("further", 1, 1), ("further", 4, 0), ("further", 3, 0), ("add", 6, 2), ("further", 2, 0), ("further", 0, 0),
    ("further", 5, 1), ("further", 1, 0), ("further", 6, 1), ("forward", 4), ("forward", 3), ("forward", 1),
    ("forward", 0), ("share_rest", 2), ("further", 6, 0), ("further", 5, 0), ("share_rest", 4), ("share_rest", 3),
    ("share_rest", 1), ("share_rest", 0), ("multiply", 2), ("multiply", 3), ("multiply", 0), ("multiply", 1),
    ("share_rest", 5), ("share_rest", 6), ("multiply", 4), ("multiply", 5), ("multiply", 6),
)


def where():
    t, e = lax.axis_index("tensor"), lax.axis_index("expert")
    return {"y": e // 8, "x": (e // 2) % 4, "z": (e % 2) * 2 + t // 2, "c": t % 2}


def device(at):
    return (at["z"] % 2) * 2 + at["c"], (at["y"] * 4 + at["x"]) * 2 + at["z"] // 2


def moved(at, axis, by):
    return {**at, axis: lax.rem(at[axis] + by, 2 if axis == "c" else SIDE)}


def send(src, dst, sems, index, at):
    copy = pltpu.make_async_remote_copy(
        src_ref=src, dst_ref=dst, send_sem=sems[0].at[index], recv_sem=sems[1].at[index],
        device_id=device(at), device_id_type=MESH,
    )
    copy.start()
    return copy


def cut(ref, fixed, rows=None, lead=(), dims="yxz", extra=()):
    tail = () if rows is None else (*extra, rows)
    return ref.at[(*lead, *(fixed.get(d, slice(None)) for d in dims), *tail)]


def sum_kernel(g_hbm, t_ref, x_ref, gap_ref, acc, rows_ref, g, f_ref, turned1, turned2, landed, q,
               stage1, sums1, stage2, sums2, stage3, local_sem, *sems):
    turn_sems, core_sems, rs_sems, ag_sems, pair_sems = (sems[2 * i:2 * i + 2] for i in range(5))
    me = where()
    c = me["c"]
    twin = moved(me, "c", 1)
    peers = [twin] + [moved(me, a, k) for a in "xyz" for k in (1, 2, 3)]
    barrier = pltpu.get_barrier_semaphore()
    for peer in peers:
        pl.semaphore_signal(barrier, inc=1, device_id=device(peer), device_id_type=MESH)
    pl.semaphore_wait(barrier, len(peers))
    sent = []

    def part_rows(p):
        return pl.ds(p * ROWS, ROWS)

    def received(copies):
        for copy in copies:
            copy.wait_recv()

    turning, moves = {}, {}

    def turned(unit, step):
        kept, started = turning.pop((unit, step), (None, ()))
        if kept is not None:
            kept.wait()
        received(started)

    def turn(unit, step):
        axis, p, lo = TURN_ORDERS[unit % 3][step], unit // 2, unit % 2
        if step:
            turned(unit, step - 1)
        place = lambda spot: {axis: spot[axis] // 2 if axis == "z" else spot[axis]}
        whole = lambda ref, fixed: cut(ref, fixed, part_rows(p), extra=(lo,))
        between = lambda ref, fixed: cut(ref, fixed, lead=(unit,))
        source = lambda fixed: between((turned1, turned2)[step - 1], fixed) if step else whole(g_hbm, fixed)
        target = lambda fixed: whole(g, fixed) if step == 2 else between((turned1, turned2)[step], fixed)
        kept = pltpu.make_async_copy(source(place(me)), target(place(me)), local_sem.at[unit * 3 + step])
        kept.start()
        started = []
        for k in (2,) if axis == "z" else (2, 1, 3):
            peer = moved(me, axis, k)
            index = unit * 9 + step * 3 + k - 1
            started.append(send(source(place(peer)), target(place(me)), turn_sems, index, peer))
        sent.extend(started)
        turning[unit, step] = kept, started

    def product(p, y, column):
        left = g[y, :, :, :, part_rows(p)].reshape(16 * ROWS, 512)
        right = t_ref[:, pl.ds(pl.multiple_of(column * HALF, HALF), HALF)]
        return jnp.dot(left, right, preferred_element_type=F32).reshape(SIDE, SIDE, ROWS, HALF)

    pairs = {}

    def pair(p):
        turned(2 * p, 2)
        turned(2 * p + 1, 2)

        @pl.loop(0, SIDE)
        def _(y):
            q[p, y] = product(p, y, 1 - c).astype(BF16)

        pairs[p] = send(q.at[p], landed.at[p], core_sems, p, twin)

    def both(p):
        pairs[p].wait_send()
        pairs[p].wait_recv()

        @pl.loop(0, SIDE)
        def _(y):
            q[p, y] = (product(p, y, c) + landed[p, y].astype(F32)).astype(BF16)

        if p in AROUND:
            around(p)
        else:
            scatter(p, 0)

    sources, slots, totals = (q, sums1, sums2), (stage1, stage2, stage3), (sums1, sums2)

    def left_after(p, step):
        return "".join(d for d in "yxz" if d not in ORDERS[p][:step])

    def scatter(p, step):
        axis, moves[p] = ORDERS[p][step], []
        for k in (2, 1, 3):
            peer = moved(me, axis, k)
            source = cut(sources[step], {axis: peer[axis]}, lead=(p,), dims=left_after(p, step))
            moves[p].append(send(source, slots[step].at[p, k - 1], rs_sems, p * 10 + step * 3 + k - 1, peer))
        sent.extend(moves[p])

    def halfway(p, at, half):
        axis, across, _ = ORDERS[p][0], *left_after(p, 1)
        return cut(q, {axis: at[axis], across: pl.ds(2 * half, 2)}, lead=(p,))

    def around(p):
        axis = ORDERS[p][0]
        moves[p] = [
            send(halfway(p, moved(me, axis, 2), half), stage1.at[p, 1, pl.ds(2 * half, 2)], rs_sems,
                 p * 10 + (1, 9)[half], moved(me, axis, k))
            for half, k in enumerate((1, 3))
        ]
        sent.extend(moves[p])

    def onward(p):
        axis, passed, moves[p] = ORDERS[p][0], moves[p], []
        for half, k in enumerate((1, 3)):
            passed[half].wait_recv()
            peer = moved(me, axis, k)
            mine = halfway(p, peer, half)
            for i in (0, 1):
                mine[i] = (mine[i].astype(F32) + stage1[p, 1, 2 * half + i].astype(F32)).astype(BF16)
            source = cut(q, {axis: peer[axis]}, lead=(p,))
            moves[p].append(send(source, stage1.at[p, k - 1], rs_sems, p * 10 + k - 1, peer))
        sent.extend(moves[p])

    def add(p, step):
        axis = ORDERS[p][step]
        ways = (0, 2) if step == 0 and p in AROUND else (0, 1, 2)
        received(moves[p])
        mine = cut(sources[step], {axis: me[axis]}, lead=(p,), dims=left_after(p, step))

        def total(at):
            value = mine[(*at,)].astype(F32)
            for k in ways:
                value += slots[step][(p, k, *at)].astype(F32)
            return value

        if step == 0:
            @pl.loop(0, SIDE)
            def _(a):
                totals[0][p, a] = total((a,))
        elif step == 1:
            totals[1][p] = total((slice(None),))
        else:
            f_ref[c, me["y"], me["x"], me["z"], part_rows(p)] = total((slice(None),)).astype(BF16)
        if step < 2:
            scatter(p, step + 1)
        else:
            gather(p, 2)

    def gather(p, step):
        part = cut(f_ref, {a: me[a] for a in ORDERS[p][:step + 1]}, part_rows(p), (c,))
        ways = (1, 3) if step == 0 and p in PASSED else (2, 1, 3)
        moves[p] = [
            send(part, part, ag_sems, p * 10 + step * 3 + k - 1, moved(me, ORDERS[p][step], k)) for k in ways
        ]
        sent.extend(moves[p])

    def further(p, step):
        received(moves[p])
        gather(p, step)
        if step == 0:
            pairs[p] = []
            share(p, 0)

    def piece(p, k, half=None):
        axis, across, _ = ORDERS[p][0], *left_after(p, 1)
        fixed = {axis: lax.rem(me[axis] + SIDE - k, SIDE)}
        if half is not None:
            fixed[across] = pl.ds(2 * half, 2)
        return cut(f_ref, fixed, part_rows(p), (c,))

    def share(p, k):
        pairs[p].append(send(piece(p, k), piece(p, k), pair_sems, p * SIDE + k, twin))
        sent.append(pairs[p][-1])

    def forward(p):
        came, moves[p] = moves[p], []
        for half, k in enumerate((1, 3)):
            came[half].wait_recv()
            part = piece(p, k, half)
            moves[p].append(send(part, part, ag_sems, p * 10 + (1, 9)[half], moved(me, ORDERS[p][0], k)))
            share(p, k)
        sent.extend(moves[p])

    def share_rest(p):
        for copy, k in zip(moves[p], (2, 2) if p in PASSED else (2, 1, 3)):
            copy.wait_recv()
            if p not in PASSED:
                share(p, k)
        if p in PASSED:
            share(p, 2)

    def multiply(p):
        received(pairs[p])
        s = jnp.concatenate([f_ref[h, :, :, :, part_rows(p)].reshape(64 * ROWS, HALF) for h in (0, 1)], axis=1)
        w = g[:, :, :, :, part_rows(p)].reshape(64 * ROWS, 512)
        acc[...] += lax.dot_general(
            s, jnp.concatenate([s, w], axis=1), (((0,), (0,)), ((), ())), preferred_element_type=F32
        )

    acc[...] = jnp.zeros_like(acc)
    steps = {f.__name__: f for f in (turn, pair, both, onward, add, further, forward, share_rest, multiply)}
    for name, *args in PLAN:
        steps[name](*args)

    for h in (0, 1):
        for lo in (0, 1):
            rows_ref[h, pl.ds(lo * CHIP_ROWS, CHIP_ROWS)] = f_ref[h, me["y"], me["x"], me["z"] // 2 * 2 + lo]
    factor(acc, x_ref, gap_ref)
    for copy in sent:
        copy.wait_send()


def dot(u, v, across=False):
    return lax.dot_general(
        u.astype(BF16), v.astype(BF16), (((1,), (1 if across else 0,)), ((), ())), preferred_element_type=F32
    )


def halves(u):
    high = u.astype(BF16)
    return high, (u - high.astype(F32)).astype(BF16)


def factor(acc, x_ref, gap_ref):
    k = acc.shape[0]
    row = lax.broadcasted_iota(jnp.int32, (k, k), 0)
    col = lax.broadcasted_iota(jnp.int32, (k, k), 1)
    eye = (row == col).astype(F32)
    half_lower = jnp.where(row > col, 1.0, 0.5 * eye)

    def change(x, gap):
        phi = (gap * half_lower).astype(BF16)
        y = dot(phi, x)
        return y - dot(phi, y)

    gram = acc[:, :k] / 7168
    diagonal = gram * eye
    down = lax.rsqrt(jnp.sum(diagonal, axis=1, keepdims=True))
    across = lax.rsqrt(jnp.sum(diagonal, axis=0, keepdims=True))
    a = gram * down * across
    high, low = halves(a)
    phi = (a - eye) * half_lower
    x = (eye - (phi - dot(phi, phi))).astype(BF16)
    x = (x.astype(F32) - change(x, dot(dot(x, high), x, True) - eye)).astype(BF16)
    left, rest = halves(dot(x, high) + dot(x, low))
    gap = dot(left, x, True) + dot(rest, x, True) - eye
    gap_ref[0, 0] = jnp.sum(gap * gap)
    x_ref[...] = (x.astype(F32) - change(x, gap)) * across


def finish_kernel(x_ref, m_ref, rows_ref, basis_ref, c_ref):
    high, low = halves(x_ref[...])
    m, m_low = halves(m_ref[...])
    c_ref[...] = (dot(high, m) + (dot(high, m_low) + dot(low, m))).astype(BF16)
    rows = jnp.concatenate([rows_ref[0], rows_ref[1]], axis=1)
    basis_ref[...] = dot(rows, high, True) + dot(rows, low, True)


def local(gate_weights, test_blocks):
    weights = gate_weights.reshape(SIDE, SIDE, 2, 2, CHIP_ROWS, 512)
    n = len(ORDERS)
    slot = lambda step, kind, *lead: pltpu.VMEM((n, *lead, *(SIDE for _ in range(3 - step)), ROWS, HALF), kind)
    turning = pltpu.VMEM((2 * n, SIDE, SIDE, 2, ROWS, 512), BF16)
    scratch = [
        pltpu.VMEM((SIDE, SIDE, 2, 2, CHIP_ROWS, 512), BF16),
        pltpu.VMEM((2, SIDE, SIDE, SIDE, CHIP_ROWS, HALF), BF16),
        turning, turning, slot(0, BF16), slot(0, BF16),
        slot(1, BF16, 3), slot(1, F32), slot(2, F32, 3), slot(2, F32), slot(3, F32, 3),
        pltpu.SemaphoreType.DMA((6 * n,)),
    ]
    for size in (18, 1, 10, 10, 4):
        scratch += [pltpu.SemaphoreType.DMA((size * n,))] * 2
    vmem, smem, hbm = (pl.BlockSpec(memory_space=m) for m in (pltpu.VMEM, pltpu.SMEM, pl.ANY))
    x, gap, acc, rows = pl.pallas_call(
        sum_kernel,
        out_shape=(
            jax.ShapeDtypeStruct((512, 512), F32),
            jax.ShapeDtypeStruct((1, 1), F32),
            jax.ShapeDtypeStruct((512, 1024), F32),
            jax.ShapeDtypeStruct((2, 224, HALF), BF16),
        ),
        in_specs=[hbm, vmem],
        out_specs=(vmem, smem, vmem, vmem),
        scratch_shapes=scratch,
        compiler_params=pltpu.CompilerParams(collective_id=0, has_side_effects=True, vmem_limit_bytes=VMEM_LIMIT),
    )(weights, test_blocks[0])

    def quick():
        return pl.pallas_call(
            finish_kernel,
            grid=(1,),
            out_shape=(jax.ShapeDtypeStruct((224, 512), F32), jax.ShapeDtypeStruct((512, 512), BF16)),
            in_specs=[
                pl.BlockSpec((512, 512), lambda i: (0, 0)),
                pl.BlockSpec((512, 512), lambda i: (0, 1)),
                pl.BlockSpec((2, 224, HALF), lambda i: (0, 0, 0)),
            ],
            out_specs=(pl.BlockSpec((224, 512), lambda i: (0, 0)), pl.BlockSpec((512, 512), lambda i: (0, 0))),
            compiler_params=pltpu.CompilerParams(vmem_limit_bytes=32 << 20),
        )(x, acc, rows)

    def exact():
        lower = jnp.linalg.cholesky(acc[:, :512] / 7168)
        x = lax.linalg.triangular_solve(lower, jnp.eye(512, dtype=F32), left_side=True, lower=True)
        high = functools.partial(jnp.dot, precision=lax.Precision.HIGHEST)
        s = jnp.concatenate([rows[0], rows[1]], axis=1).astype(F32)
        return high(s, x.T), high(x, acc[:, 512:]).astype(BF16)

    basis, coefficients = lax.cond(gap[0, 0] < 0.1, quick, exact)
    return basis, coefficients[None]


def solution(mesh):
    placed = (P(None, "expert", "tensor"), P("expert", "tensor", None))
    return jax.shard_map(
        local,
        mesh=mesh,
        in_specs=placed,
        out_specs=(P("expert", None), P("expert", None, "tensor")),
        check_vma=False,
    )
```

```python
import functools

import jax
import jax.numpy as jnp
from jax import lax
from jax.experimental import pallas as pl
from jax.experimental.pallas import tpu as pltpu
from jax.sharding import PartitionSpec as P

MESH = pl.DeviceIdType.MESH
F32, BF16 = jnp.float32, jnp.bfloat16
SIDE = 4
CHIP_ROWS = 112
HALF = 256
LANES = 128
VMEM_LIMIT = 62 << 20
ROWS = 16
ORDERS = ("xzy", "xyz", "yxz", "yzx", "xyz", "yxz", "zxy", "xyz", "zxy", "zyx", "zxy", "yxz", "zyx", "yxz")
AROUND = (2, 3, 7, 8, 11, 12, 13)
PASSED = (0, 1, 4, 5, 6, 10)
TURN_ORDERS = ("xyz", "yzx", "zxy")
PLAN = (
    ("turn", 0, 0), ("turn", 1, 0), ("turn", 2, 0), ("turn", 3, 0), ("turn", 4, 0), ("turn", 5, 0), ("turn", 6, 0),
    ("turn", 7, 0), ("turn", 8, 0), ("turn", 9, 0), ("turn", 10, 0), ("turn", 11, 0), ("turn", 12, 0), ("turn", 13, 0),
    ("turn", 1, 1), ("turn", 2, 1), ("turn", 0, 1), ("turn", 4, 1), ("turn", 5, 1), ("turn", 3, 1), ("turn", 7, 1),
    ("turn", 8, 1), ("turn", 6, 1), ("turn", 10, 1), ("turn", 11, 1), ("turn", 9, 1), ("turn", 13, 1), ("turn", 1, 2),
    ("turn", 12, 1), ("turn", 0, 2), ("turn", 4, 2), ("turn", 2, 2), ("turn", 3, 2), ("turn", 7, 2), ("turn", 5, 2),
    ("turn", 6, 2), ("turn", 10, 2), ("turn", 8, 2), ("turn", 9, 2), ("turn", 13, 2), ("turn", 11, 2), ("pair", 0),
    ("turn", 12, 2), ("both", 0), ("pair", 1), ("both", 1), ("pair", 2), ("pair", 3), ("both", 2), ("both", 3),
    ("pair", 4), ("both", 4), ("pair", 5), ("pair", 6), ("onward", 2), ("onward", 3), ("add", 0, 0), ("both", 5),
    ("both", 6), ("add", 5, 0), ("add", 6, 0), ("onward", 8), ("add", 1, 0), ("add", 2, 0), ("add", 9, 0),
    ("add", 3, 0), ("add", 0, 1), ("add", 4, 0), ("onward", 11), ("onward", 7), ("onward", 13), ("add", 5, 1),
    ("add", 1, 1), ("add", 10, 0), ("onward", 12), ("add", 6, 1), ("add", 9, 1), ("add", 0, 2), ("add", 8, 0),
    ("add", 2, 1), ("add", 4, 1), ("add", 3, 1), ("add", 5, 2), ("add", 7, 0), ("add", 1, 2), ("add", 11, 0),
    ("add", 10, 1), ("add", 12, 0), ("add", 9, 2), ("add", 13, 0), ("add", 2, 2), ("add", 6, 2), ("further", 0, 1),
    ("add", 4, 2), ("further", 5, 1), ("add", 8, 1), ("further", 1, 1), ("add", 3, 2), ("add", 7, 1), ("add", 10, 2),
    ("add", 11, 1), ("further", 9, 1), ("further", 2, 1), ("further", 0, 0), ("further", 4, 1), ("add", 12, 1),
    ("further", 6, 1), ("add", 13, 1), ("add", 8, 2), ("further", 5, 0), ("further", 3, 1), ("further", 1, 0),
    ("add", 7, 2), ("further", 10, 1), ("add", 11, 2), ("further", 9, 0), ("further", 2, 0), ("further", 4, 0),
    ("further", 8, 1), ("add", 13, 2), ("forward", 0), ("add", 12, 2), ("further", 3, 0), ("further", 7, 1),
    ("further", 11, 1), ("further", 6, 0), ("forward", 5), ("forward", 1), ("further", 10, 0), ("share_rest", 9),
    ("further", 13, 1), ("share_rest", 2), ("forward", 4), ("further", 8, 0), ("forward", 6), ("share_rest", 0),
    ("further", 12, 1), ("further", 11, 0), ("share_rest", 3), ("forward", 10), ("share_rest", 1), ("further", 7, 0),
    ("further", 13, 0), ("share_rest", 5), ("share_rest", 4), ("multiply", 0), ("further", 12, 0), ("multiply", 1),
    ("share_rest", 8), ("share_rest", 6), ("multiply", 2), ("share_rest", 10), ("share_rest", 11), ("multiply", 4),
    ("share_rest", 7), ("multiply", 5), ("share_rest", 13), ("share_rest", 12), ("multiply", 3), ("multiply", 6),
)


def where():
    t, e = lax.axis_index("tensor"), lax.axis_index("expert")
    return {"y": e // 8, "x": (e // 2) % 4, "z": (e % 2) * 2 + t // 2, "c": t % 2}


def device(at):
    return (at["z"] % 2) * 2 + at["c"], (at["y"] * 4 + at["x"]) * 2 + at["z"] // 2


def moved(at, axis, by):
    return {**at, axis: lax.rem(at[axis] + by, 2 if axis == "c" else SIDE)}


def send(src, dst, sems, index, at):
    copy = pltpu.make_async_remote_copy(
        src_ref=src, dst_ref=dst, send_sem=sems[0].at[index], recv_sem=sems[1].at[index],
        device_id=device(at), device_id_type=MESH,
    )
    copy.start()
    return copy


def cut(ref, fixed, rows=None, lead=(), dims="yxz", extra=()):
    tail = () if rows is None else (*extra, rows)
    return ref.at[(*lead, *(fixed.get(d, slice(None)) for d in dims), *tail)]


def sum_kernel(g_hbm, t_hbm, x_ref, gap_ref, acc_hbm, rows_ref, t_ref, acc, g, f_ref, turned1, turned2, landed, q,
               stage1, sums1, stage2, sums2, stage3, own_sem, local_sem, *sems):
    turn_sems, core_sems, rs_sems, ag_sems, pair_sems = (sems[2 * i:2 * i + 2] for i in range(5))
    load = pltpu.make_async_copy(t_hbm, t_ref, own_sem.at[0])
    load.start()
    me = where()
    c = me["c"]
    twin = moved(me, "c", 1)
    peers = [twin] + [moved(me, a, k) for a in "xyz" for k in (1, 2, 3)]
    barrier = pltpu.get_barrier_semaphore()
    for peer in peers:
        pl.semaphore_signal(barrier, inc=1, device_id=device(peer), device_id_type=MESH)
    pl.semaphore_wait(barrier, len(peers))
    sent = []

    def part_rows(p):
        return pl.ds(p * ROWS, ROWS)

    def received(copies):
        for copy in copies:
            copy.wait_recv()

    turning, moves = {}, {}

    def turned(unit, step):
        kept, started = turning.pop((unit, step), (None, ()))
        if kept is not None:
            kept.wait()
        received(started)

    def turn(unit, step):
        axis, p, lo = TURN_ORDERS[unit % 3][step], unit // 2, unit % 2
        if step:
            turned(unit, step - 1)
        place = lambda spot: {axis: spot[axis] // 2 if axis == "z" else spot[axis]}
        between = lambda ref, fixed: cut(ref, fixed, lead=(unit,))
        first = lambda fixed: cut(g_hbm, fixed, part_rows(p), extra=(lo,))
        last = lambda fixed: cut(g, fixed, lead=(p,), extra=(lo,), rows=slice(None))
        source = lambda fixed: between((turned1, turned2)[step - 1], fixed) if step else first(fixed)
        target = lambda fixed: last(fixed) if step == 2 else between((turned1, turned2)[step], fixed)
        kept = pltpu.make_async_copy(source(place(me)), target(place(me)), local_sem.at[unit * 3 + step])
        kept.start()
        started = []
        for k in (2,) if axis == "z" else (2, 1, 3):
            peer = moved(me, axis, k)
            index = unit * 9 + step * 3 + k - 1
            started.append(send(source(place(peer)), target(place(me)), turn_sems, index, peer))
        sent.extend(started)
        turning[unit, step] = kept, started

    def product(p, y, column):
        left = g[p, y].reshape(16 * ROWS, 512)
        right = t_ref[:, pl.ds(pl.multiple_of(column * HALF, HALF), HALF)]
        return jnp.dot(left, right, preferred_element_type=F32).reshape(SIDE, SIDE, ROWS, HALF)

    pairs, shares = {}, {}

    def pair(p):
        turned(2 * p, 2)
        turned(2 * p + 1, 2)

        @pl.loop(0, SIDE)
        def _(y):
            value = product(p, y, 1 - c).astype(BF16)
            for h in (0, 1):
                q[2 * p + h, y] = value[..., h * LANES:(h + 1) * LANES]

        units = pl.ds(2 * p, 2)
        pairs[p] = send(q.at[units], landed.at[units], core_sems, p, twin)

    def both(p):
        pairs[p].wait_send()
        pairs[p].wait_recv()

        @pl.loop(0, SIDE)
        def _(y):
            value = product(p, y, c)
            for h in (0, 1):
                unit = 2 * p + h
                part = value[..., h * LANES:(h + 1) * LANES]
                q[unit, y] = (part + landed[unit, y].astype(F32)).astype(BF16)

        for unit in (2 * p, 2 * p + 1):
            if unit in AROUND:
                around(unit)
            else:
                scatter(unit, 0)

    sources, slots, totals = (q, sums1, sums2), (stage1, stage2, stage3), (sums1, sums2)

    def left_after(p, step):
        return "".join(d for d in "yxz" if d not in ORDERS[p][:step])

    def scatter(p, step):
        axis, moves[p] = ORDERS[p][step], []
        for k in (2, 1, 3):
            peer = moved(me, axis, k)
            source = cut(sources[step], {axis: peer[axis]}, lead=(p,), dims=left_after(p, step))
            moves[p].append(send(source, slots[step].at[p, k - 1], rs_sems, p * 10 + step * 3 + k - 1, peer))
        sent.extend(moves[p])

    def halfway(p, at, half):
        axis, across, _ = ORDERS[p][0], *left_after(p, 1)
        return cut(q, {axis: at[axis], across: pl.ds(2 * half, 2)}, lead=(p,))

    def around(p):
        axis = ORDERS[p][0]
        moves[p] = [
            send(halfway(p, moved(me, axis, 2), half), stage1.at[p, 1, pl.ds(2 * half, 2)], rs_sems,
                 p * 10 + (1, 9)[half], moved(me, axis, k))
            for half, k in enumerate((1, 3))
        ]
        sent.extend(moves[p])

    def onward(p):
        axis, passed, moves[p] = ORDERS[p][0], moves[p], []
        for half, k in enumerate((1, 3)):
            passed[half].wait_recv()
            peer = moved(me, axis, k)
            mine = halfway(p, peer, half)
            for i in (0, 1):
                mine[i] = (mine[i].astype(F32) + stage1[p, 1, 2 * half + i].astype(F32)).astype(BF16)
            source = cut(q, {axis: peer[axis]}, lead=(p,))
            moves[p].append(send(source, stage1.at[p, k - 1], rs_sems, p * 10 + k - 1, peer))
        sent.extend(moves[p])

    def add(p, step):
        axis = ORDERS[p][step]
        ways = (0, 2) if step == 0 and p in AROUND else (0, 1, 2)
        received(moves[p])
        mine = cut(sources[step], {axis: me[axis]}, lead=(p,), dims=left_after(p, step))

        def total(at):
            value = mine[(*at,)].astype(F32)
            for k in ways:
                value += slots[step][(p, k, *at)].astype(F32)
            return value

        if step == 0:
            @pl.loop(0, SIDE)
            def _(a):
                totals[0][p, a] = total((a,))
        elif step == 1:
            totals[1][p] = total((slice(None),))
        else:
            f_ref[c, p, me["y"], me["x"], me["z"]] = total((slice(None),)).astype(BF16)
        if step < 2:
            scatter(p, step + 1)
        else:
            gather(p, 2)

    def gather(p, step):
        part = cut(f_ref, {a: me[a] for a in ORDERS[p][:step + 1]}, lead=(c, p))
        ways = (1, 3) if step == 0 and p in PASSED else (2, 1, 3)
        moves[p] = [
            send(part, part, ag_sems, p * 10 + step * 3 + k - 1, moved(me, ORDERS[p][step], k)) for k in ways
        ]
        sent.extend(moves[p])

    def further(p, step):
        received(moves[p])
        gather(p, step)
        if step == 0:
            shares[p] = []
            share(p, 0)

    def piece(p, k, half=None):
        axis, across, _ = ORDERS[p][0], *left_after(p, 1)
        fixed = {axis: lax.rem(me[axis] + SIDE - k, SIDE)}
        if half is not None:
            fixed[across] = pl.ds(2 * half, 2)
        return cut(f_ref, fixed, lead=(c, p))

    def share(p, k):
        shares[p].append(send(piece(p, k), piece(p, k), pair_sems, p * SIDE + k, twin))
        sent.append(shares[p][-1])

    def forward(p):
        came, moves[p] = moves[p], []
        for half, k in enumerate((1, 3)):
            came[half].wait_recv()
            part = piece(p, k, half)
            moves[p].append(send(part, part, ag_sems, p * 10 + (1, 9)[half], moved(me, ORDERS[p][0], k)))
            share(p, k)
        sent.extend(moves[p])

    def share_rest(p):
        for copy, k in zip(moves[p], (2, 2) if p in PASSED else (2, 1, 3)):
            copy.wait_recv()
            if p not in PASSED:
                share(p, k)
        if p in PASSED:
            share(p, 2)

    def multiply(p):
        units = (2 * p, 2 * p + 1)
        for unit in units:
            received(shares[unit])
        s = jnp.concatenate([f_ref[h, unit].reshape(64 * ROWS, LANES) for h in (0, 1) for unit in units], axis=1)
        w = g[p].reshape(64 * ROWS, 512)
        acc[...] += lax.dot_general(
            s, jnp.concatenate([s, w], axis=1), (((0,), (0,)), ((), ())), preferred_element_type=F32
        )

    acc[...] = jnp.zeros_like(acc)
    load.wait()
    steps = {f.__name__: f for f in (turn, pair, both, onward, add, further, forward, share_rest, multiply)}
    for name, *args in PLAN:
        steps[name](*args)

    for core in (0, 1):
        for lo in (0, 1):
            for unit in range(len(ORDERS)):
                at, lanes = pl.ds(lo * CHIP_ROWS + unit // 2 * ROWS, ROWS), pl.ds(unit % 2 * LANES, LANES)
                rows_ref[core, at, lanes] = f_ref[core, unit, me["y"], me["x"], me["z"] // 2 * 2 + lo]
    store = pltpu.make_async_copy(acc, acc_hbm, own_sem.at[1])
    store.start()
    factor(acc, x_ref, gap_ref)
    store.wait()
    for copy in sent:
        copy.wait_send()


def dot(u, v, across=False):
    return lax.dot_general(
        u.astype(BF16), v.astype(BF16), (((1,), (1 if across else 0,)), ((), ())), preferred_element_type=F32
    )


def halves(u):
    high = u.astype(BF16)
    return high, (u - high.astype(F32)).astype(BF16)


def factor(acc, x_ref, gap_ref):
    k = acc.shape[0]
    row = lax.broadcasted_iota(jnp.int32, (k, k), 0)
    col = lax.broadcasted_iota(jnp.int32, (k, k), 1)
    eye = (row == col).astype(F32)
    half_lower = jnp.where(row > col, 1.0, 0.5 * eye)

    def change(x, gap):
        phi = (gap * half_lower).astype(BF16)
        y = dot(phi, x)
        return y - dot(phi, y)

    gram = acc[:, :k] / 7168
    diagonal = gram * eye
    down = lax.rsqrt(jnp.sum(diagonal, axis=1, keepdims=True))
    across = lax.rsqrt(jnp.sum(diagonal, axis=0, keepdims=True))
    a = gram * down * across
    high, low = halves(a)
    phi = (a - eye) * half_lower
    x = (eye - (phi - dot(phi, phi))).astype(BF16)
    x = (x.astype(F32) - change(x, dot(dot(x, high), x, True) - eye)).astype(BF16)
    left, rest = halves(dot(x, high) + dot(x, low))
    gap = dot(left, x, True) + dot(rest, x, True) - eye
    gap_ref[0, 0] = jnp.sum(gap * gap)
    x_ref[...] = (x.astype(F32) - change(x, gap)) * across


def finish_kernel(x_ref, m_ref, rows_ref, basis_ref, c_ref):
    high, low = halves(x_ref[...])
    m, m_low = halves(m_ref[...])
    c_ref[...] = (dot(high, m) + (dot(high, m_low) + dot(low, m))).astype(BF16)
    rows = jnp.concatenate([rows_ref[0], rows_ref[1]], axis=1)
    basis_ref[...] = dot(rows, high, True) + dot(rows, low, True)


def local(gate_weights, test_blocks):
    weights = gate_weights.reshape(SIDE, SIDE, 2, 2, CHIP_ROWS, 512)
    n = len(ORDERS) // 2
    slot = lambda step, kind, *lead: pltpu.VMEM((2 * n, *lead, *(SIDE for _ in range(3 - step)), ROWS, LANES), kind)
    turning = pltpu.VMEM((2 * n, SIDE, SIDE, 2, ROWS, 512), BF16)
    scratch = [
        pltpu.VMEM((512, 512), BF16),
        pltpu.VMEM((512, 1024), F32),
        pltpu.VMEM((n, SIDE, SIDE, 2, 2, ROWS, 512), BF16),
        pltpu.VMEM((2, 2 * n, SIDE, SIDE, SIDE, ROWS, LANES), BF16),
        turning, turning, slot(0, BF16), slot(0, BF16),
        slot(1, BF16, 3), slot(1, F32), slot(2, F32, 3), slot(2, F32), slot(3, F32, 3),
        pltpu.SemaphoreType.DMA((2,)),
        pltpu.SemaphoreType.DMA((6 * n,)),
    ]
    for size in (18, 1, 20, 20, 8):
        scratch += [pltpu.SemaphoreType.DMA((size * n,))] * 2
    vmem, smem, hbm = (pl.BlockSpec(memory_space=m) for m in (pltpu.VMEM, pltpu.SMEM, pl.ANY))
    x, gap, acc, rows = pl.pallas_call(
        sum_kernel,
        out_shape=(
            jax.ShapeDtypeStruct((512, 512), F32),
            jax.ShapeDtypeStruct((1, 1), F32),
            jax.ShapeDtypeStruct((512, 1024), F32),
            jax.ShapeDtypeStruct((2, 224, HALF), BF16),
        ),
        in_specs=[hbm, hbm],
        out_specs=(vmem, smem, hbm, vmem),
        scratch_shapes=scratch,
        compiler_params=pltpu.CompilerParams(collective_id=0, has_side_effects=True, vmem_limit_bytes=VMEM_LIMIT),
    )(weights, test_blocks[0])

    def quick():
        return pl.pallas_call(
            finish_kernel,
            grid=(1,),
            out_shape=(jax.ShapeDtypeStruct((224, 512), F32), jax.ShapeDtypeStruct((512, 512), BF16)),
            in_specs=[
                pl.BlockSpec((512, 512), lambda i: (0, 0)),
                pl.BlockSpec((512, 512), lambda i: (0, 1)),
                pl.BlockSpec((2, 224, HALF), lambda i: (0, 0, 0)),
            ],
            out_specs=(pl.BlockSpec((224, 512), lambda i: (0, 0)), pl.BlockSpec((512, 512), lambda i: (0, 0))),
            compiler_params=pltpu.CompilerParams(vmem_limit_bytes=32 << 20),
        )(x, acc, rows)

    def exact():
        lower = jnp.linalg.cholesky(acc[:, :512] / 7168)
        x = lax.linalg.triangular_solve(lower, jnp.eye(512, dtype=F32), left_side=True, lower=True)
        high = functools.partial(jnp.dot, precision=lax.Precision.HIGHEST)
        s = jnp.concatenate([rows[0], rows[1]], axis=1).astype(F32)
        return high(s, x.T), high(x, acc[:, 512:]).astype(BF16)

    basis, coefficients = lax.cond(gap[0, 0] < 0.1, quick, exact)
    return basis, coefficients[None]


def solution(mesh):
    placed = (P(None, "expert", "tensor"), P("expert", "tensor", None))
    return jax.shard_map(
        local,
        mesh=mesh,
        in_specs=placed,
        out_specs=(P("expert", None), P("expert", None, "tensor")),
        check_vma=False,
    )
```

```python
import functools

import jax
import jax.numpy as jnp
from jax import lax
from jax.experimental import pallas as pl
from jax.experimental.pallas import tpu as pltpu
from jax.sharding import PartitionSpec as P

MESH = pl.DeviceIdType.MESH
F32, BF16 = jnp.float32, jnp.bfloat16
SIDE = 4
CHIP_ROWS = 112
HALF = 256
LANES = 128
VMEM_LIMIT = 62 << 20
ROWS = 16
ORDERS = ("xzy", "xyz", "yxz", "yzx", "xyz", "yxz", "zxy", "xyz", "zxy", "zyx", "zxy", "yxz", "zyx", "yxz")
AROUND = (2, 3, 7, 8, 11, 12, 13)
PASSED = (0, 1, 4, 5, 6, 10)
TURN_ORDERS = ("xyz", "yzx", "zxy")
PLAN = (
    ("turn", 0, 0), ("turn", 1, 0), ("turn", 2, 0), ("turn", 3, 0), ("turn", 4, 0), ("turn", 5, 0), ("turn", 6, 0),
    ("turn", 7, 0), ("turn", 8, 0), ("turn", 9, 0), ("turn", 10, 0), ("turn", 11, 0), ("turn", 12, 0), ("turn", 13, 0),
    ("turn", 1, 1), ("turn", 2, 1), ("turn", 0, 1), ("turn", 4, 1), ("turn", 5, 1), ("turn", 3, 1), ("turn", 7, 1),
    ("turn", 8, 1), ("turn", 6, 1), ("turn", 10, 1), ("turn", 11, 1), ("turn", 9, 1), ("turn", 13, 1), ("turn", 1, 2),
    ("turn", 12, 1), ("turn", 0, 2), ("turn", 4, 2), ("turn", 2, 2), ("turn", 3, 2), ("turn", 7, 2), ("turn", 5, 2),
    ("turn", 6, 2), ("turn", 10, 2), ("turn", 8, 2), ("turn", 9, 2), ("turn", 13, 2), ("turn", 11, 2), ("pair", 0),
    ("turn", 12, 2), ("both", 0), ("pair", 1), ("both", 1), ("pair", 2), ("pair", 3), ("both", 2), ("both", 3),
    ("pair", 4), ("both", 4), ("pair", 5), ("pair", 6), ("onward", 2), ("onward", 3), ("add", 0, 0), ("both", 5),
    ("both", 6), ("add", 5, 0), ("add", 6, 0), ("onward", 8), ("add", 1, 0), ("add", 2, 0), ("add", 9, 0),
    ("add", 3, 0), ("add", 0, 1), ("add", 4, 0), ("onward", 11), ("onward", 7), ("onward", 13), ("add", 5, 1),
    ("add", 1, 1), ("add", 10, 0), ("onward", 12), ("add", 6, 1), ("add", 9, 1), ("add", 0, 2), ("add", 8, 0),
    ("add", 2, 1), ("add", 4, 1), ("add", 3, 1), ("add", 5, 2), ("add", 7, 0), ("add", 1, 2), ("add", 11, 0),
    ("add", 10, 1), ("add", 12, 0), ("add", 9, 2), ("add", 13, 0), ("add", 2, 2), ("add", 6, 2), ("further", 0, 1),
    ("add", 4, 2), ("further", 5, 1), ("add", 8, 1), ("further", 1, 1), ("add", 3, 2), ("add", 7, 1), ("add", 10, 2),
    ("add", 11, 1), ("further", 9, 1), ("further", 2, 1), ("further", 0, 0), ("further", 4, 1), ("add", 12, 1),
    ("further", 6, 1), ("add", 13, 1), ("add", 8, 2), ("further", 5, 0), ("further", 3, 1), ("further", 1, 0),
    ("add", 7, 2), ("further", 10, 1), ("add", 11, 2), ("further", 9, 0), ("further", 2, 0), ("further", 4, 0),
    ("further", 8, 1), ("add", 13, 2), ("forward", 0), ("add", 12, 2), ("further", 3, 0), ("further", 7, 1),
    ("further", 11, 1), ("further", 6, 0), ("forward", 5), ("forward", 1), ("further", 10, 0), ("share_rest", 9),
    ("further", 13, 1), ("share_rest", 2), ("forward", 4), ("further", 8, 0), ("forward", 6), ("share_rest", 0),
    ("further", 12, 1), ("further", 11, 0), ("share_rest", 3), ("forward", 10), ("share_rest", 1), ("further", 7, 0),
    ("further", 13, 0), ("share_rest", 5), ("share_rest", 4), ("multiply", 0), ("further", 12, 0), ("multiply", 1),
    ("share_rest", 8), ("share_rest", 6), ("multiply", 2), ("share_rest", 10), ("share_rest", 11), ("multiply", 4),
    ("share_rest", 7), ("multiply", 5), ("share_rest", 13), ("share_rest", 12), ("multiply", 3), ("multiply", 6),
)


def where():
    t, e = lax.axis_index("tensor"), lax.axis_index("expert")
    return {"y": e // 8, "x": (e // 2) % 4, "z": (e % 2) * 2 + t // 2, "c": t % 2}


def device(at):
    return (at["z"] % 2) * 2 + at["c"], (at["y"] * 4 + at["x"]) * 2 + at["z"] // 2


def moved(at, axis, by):
    return {**at, axis: lax.rem(at[axis] + by, 2 if axis == "c" else SIDE)}


def send(src, dst, sems, index, at):
    copy = pltpu.make_async_remote_copy(
        src_ref=src, dst_ref=dst, send_sem=sems[0].at[index], recv_sem=sems[1].at[index],
        device_id=device(at), device_id_type=MESH,
    )
    copy.start()
    return copy


def cut(ref, fixed, rows=None, lead=(), dims="yxz", extra=()):
    tail = () if rows is None else (*extra, rows)
    return ref.at[(*lead, *(fixed.get(d, slice(None)) for d in dims), *tail)]


def sum_kernel(g_hbm, t_hbm, x_ref, gap_ref, acc_hbm, rows_ref, t_ref, acc, g, f_ref, turned1, turned2, landed, q,
               stage1, sums1, stage2, sums2, stage3, own_sem, local_sem, *sems):
    turn_sems, core_sems, rs_sems, ag_sems, pair_sems = (sems[2 * i:2 * i + 2] for i in range(5))
    load = pltpu.make_async_copy(t_hbm, t_ref, own_sem.at[0])
    load.start()
    me = where()
    c = me["c"]
    twin = moved(me, "c", 1)
    peers = [twin] + [moved(me, a, k) for a in "xyz" for k in (1, 2, 3)]
    barrier = pltpu.get_barrier_semaphore()
    for peer in peers:
        pl.semaphore_signal(barrier, inc=1, device_id=device(peer), device_id_type=MESH)
    pl.semaphore_wait(barrier, len(peers))
    sent = []

    def part_rows(p):
        return pl.ds(p * ROWS, ROWS)

    def received(copies):
        for copy in copies:
            copy.wait_recv()

    turning, moves = {}, {}

    def turned(unit, step):
        kept, started = turning.pop((unit, step), (None, ()))
        if kept is not None:
            kept.wait()
        received(started)

    def turn(unit, step):
        axis, p, lo = TURN_ORDERS[unit % 3][step], unit // 2, unit % 2
        if step:
            turned(unit, step - 1)
        place = lambda spot: {axis: spot[axis] // 2 if axis == "z" else spot[axis]}
        between = lambda ref, fixed: cut(ref, fixed, lead=(unit,))
        first = lambda fixed: cut(g_hbm, fixed, part_rows(p), extra=(lo,))
        last = lambda fixed: cut(g, fixed, lead=(p,), extra=(lo,), rows=slice(None))
        source = lambda fixed: between((turned1, turned2)[step - 1], fixed) if step else first(fixed)
        target = lambda fixed: last(fixed) if step == 2 else between((turned1, turned2)[step], fixed)
        kept = pltpu.make_async_copy(source(place(me)), target(place(me)), local_sem.at[unit * 3 + step])
        kept.start()
        started = []
        for k in (2,) if axis == "z" else (2, 1, 3):
            peer = moved(me, axis, k)
            index = unit * 9 + step * 3 + k - 1
            started.append(send(source(place(peer)), target(place(me)), turn_sems, index, peer))
        sent.extend(started)
        turning[unit, step] = kept, started

    def product(p, y, column):
        left = g[p, y].reshape(16 * ROWS, 512)
        right = t_ref[:, pl.ds(pl.multiple_of(column * HALF, HALF), HALF)]
        return jnp.dot(left, right, preferred_element_type=F32).reshape(SIDE, SIDE, ROWS, HALF)

    pairs, shares = {}, {}

    def pair(p):
        turned(2 * p, 2)
        turned(2 * p + 1, 2)

        @pl.loop(0, SIDE)
        def _(y):
            value = product(p, y, 1 - c).astype(BF16)
            for h in (0, 1):
                q[2 * p + h, y] = value[..., h * LANES:(h + 1) * LANES]

        units = pl.ds(2 * p, 2)
        pairs[p] = send(q.at[units], landed.at[units], core_sems, p, twin)

    def both(p):
        pairs[p].wait_send()
        pairs[p].wait_recv()

        @pl.loop(0, SIDE)
        def _(y):
            value = product(p, y, c)
            for h in (0, 1):
                unit = 2 * p + h
                part = value[..., h * LANES:(h + 1) * LANES]
                q[unit, y] = (part + landed[unit, y].astype(F32)).astype(BF16)

        for unit in (2 * p, 2 * p + 1):
            if unit in AROUND:
                around(unit)
            else:
                scatter(unit, 0)

    sources, slots, totals = (q, sums1, sums2), (stage1, stage2, stage3), (sums1, sums2)

    def left_after(p, step):
        return "".join(d for d in "yxz" if d not in ORDERS[p][:step])

    def scatter(p, step):
        axis, moves[p] = ORDERS[p][step], []
        for k in (2, 1, 3):
            peer = moved(me, axis, k)
            source = cut(sources[step], {axis: peer[axis]}, lead=(p,), dims=left_after(p, step))
            moves[p].append(send(source, slots[step].at[p, k - 1], rs_sems, p * 10 + step * 3 + k - 1, peer))
        sent.extend(moves[p])

    def halfway(p, at, half):
        axis, across, _ = ORDERS[p][0], *left_after(p, 1)
        return cut(q, {axis: at[axis], across: pl.ds(2 * half, 2)}, lead=(p,))

    def around(p):
        axis = ORDERS[p][0]
        moves[p] = [
            send(halfway(p, moved(me, axis, 2), half), stage1.at[p, 1, pl.ds(2 * half, 2)], rs_sems,
                 p * 10 + (1, 9)[half], moved(me, axis, k))
            for half, k in enumerate((1, 3))
        ]
        sent.extend(moves[p])

    def onward(p):
        axis, passed, moves[p] = ORDERS[p][0], moves[p], []
        for half, k in enumerate((1, 3)):
            passed[half].wait_recv()
            peer = moved(me, axis, k)
            mine = halfway(p, peer, half)
            for i in (0, 1):
                mine[i] = (mine[i].astype(F32) + stage1[p, 1, 2 * half + i].astype(F32)).astype(BF16)
            source = cut(q, {axis: peer[axis]}, lead=(p,))
            moves[p].append(send(source, stage1.at[p, k - 1], rs_sems, p * 10 + k - 1, peer))
        sent.extend(moves[p])

    def add(p, step):
        axis = ORDERS[p][step]
        ways = (0, 2) if step == 0 and p in AROUND else (0, 1, 2)
        received(moves[p])
        mine = cut(sources[step], {axis: me[axis]}, lead=(p,), dims=left_after(p, step))

        def total(at):
            value = mine[(*at,)].astype(F32)
            for k in ways:
                value += slots[step][(p, k, *at)].astype(F32)
            return value

        if step == 0:
            @pl.loop(0, SIDE)
            def _(a):
                totals[0][p, a] = total((a,))
        elif step == 1:
            totals[1][p] = total((slice(None),))
        else:
            f_ref[c, p, me["y"], me["x"], me["z"]] = total((slice(None),)).astype(BF16)
        if step < 2:
            scatter(p, step + 1)
        else:
            gather(p, 2)

    def gather(p, step):
        part = cut(f_ref, {a: me[a] for a in ORDERS[p][:step + 1]}, lead=(c, p))
        ways = (1, 3) if step == 0 and p in PASSED else (2, 1, 3)
        moves[p] = [
            send(part, part, ag_sems, p * 10 + step * 3 + k - 1, moved(me, ORDERS[p][step], k)) for k in ways
        ]
        sent.extend(moves[p])

    def further(p, step):
        received(moves[p])
        gather(p, step)
        if step == 0:
            shares[p] = []
            share(p, 0)

    def piece(p, k, half=None):
        axis, across, _ = ORDERS[p][0], *left_after(p, 1)
        fixed = {axis: lax.rem(me[axis] + SIDE - k, SIDE)}
        if half is not None:
            fixed[across] = pl.ds(2 * half, 2)
        return cut(f_ref, fixed, lead=(c, p))

    def share(p, k):
        shares[p].append(send(piece(p, k), piece(p, k), pair_sems, p * SIDE + k, twin))
        sent.append(shares[p][-1])

    def forward(p):
        came, moves[p] = moves[p], []
        for half, k in enumerate((1, 3)):
            came[half].wait_recv()
            part = piece(p, k, half)
            moves[p].append(send(part, part, ag_sems, p * 10 + (1, 9)[half], moved(me, ORDERS[p][0], k)))
            share(p, k)
        sent.extend(moves[p])

    def share_rest(p):
        for copy, k in zip(moves[p], (2, 2) if p in PASSED else (2, 1, 3)):
            copy.wait_recv()
            if p not in PASSED:
                share(p, k)
        if p in PASSED:
            share(p, 2)

    def multiply(p):
        units = (2 * p, 2 * p + 1)
        for unit in units:
            received(shares[unit])
        s = jnp.concatenate([f_ref[h, unit].reshape(64 * ROWS, LANES) for h in (0, 1) for unit in units], axis=1)
        w = g[p].reshape(64 * ROWS, 512)
        acc[...] += lax.dot_general(
            s, jnp.concatenate([s, w], axis=1), (((0,), (0,)), ((), ())), preferred_element_type=F32
        )

    acc[...] = jnp.zeros_like(acc)
    load.wait()
    steps = {f.__name__: f for f in (turn, pair, both, onward, add, further, forward, share_rest, multiply)}
    for name, *args in PLAN:
        steps[name](*args)

    for core in (0, 1):
        for lo in (0, 1):
            for unit in range(len(ORDERS)):
                at, lanes = pl.ds(lo * CHIP_ROWS + unit // 2 * ROWS, ROWS), pl.ds(unit % 2 * LANES, LANES)
                rows_ref[core, at, lanes] = f_ref[core, unit, me["y"], me["x"], me["z"] // 2 * 2 + lo]
    store = pltpu.make_async_copy(acc, acc_hbm, own_sem.at[1])
    store.start()
    factor(acc, x_ref, gap_ref)
    store.wait()
    for copy in sent:
        copy.wait_send()


def dot(u, v, across=False):
    return lax.dot_general(
        u.astype(BF16), v.astype(BF16), (((1,), (1 if across else 0,)), ((), ())), preferred_element_type=F32
    )


def halves(u):
    high = u.astype(BF16)
    return high, (u - high.astype(F32)).astype(BF16)


def factor(acc, x_ref, gap_ref):
    k = acc.shape[0]
    h = k // 2
    spots = ((0, 0), (1, 0), (1, 1))
    part = lambda u, i, j: u[i * h:(i + 1) * h, j * h:(j + 1) * h]
    blocks = lambda f, *us: {at: f(*(u[at] for u in us)) for at in spots}
    row = lax.broadcasted_iota(jnp.int32, (h, h), 0)
    col = lax.broadcasted_iota(jnp.int32, (h, h), 1)
    one = (row == col).astype(F32)
    half = jnp.where(row > col, 1.0, 0.5 * one)
    eye = {(0, 0): one, (1, 0): jnp.zeros_like(one), (1, 1): one}
    half_lower = {(0, 0): half, (1, 0): jnp.ones_like(one), (1, 1): half}
    minus = lambda u, v: u - v
    times = lambda u, v: u * v
    half_precise = lambda u: u.astype(BF16)

    def lower_lower(u, v):
        return {
            (0, 0): dot(u[0, 0], v[0, 0]),
            (1, 0): dot(u[1, 0], v[0, 0]) + dot(u[1, 1], v[1, 0]),
            (1, 1): dot(u[1, 1], v[1, 1]),
        }

    def lower_whole(u, v):
        return {
            (0, 0): dot(u[0, 0], part(v, 0, 0)),
            (1, 0): dot(u[1, 0], part(v, 0, 0)) + dot(u[1, 1], part(v, 1, 0)),
            (1, 1): dot(u[1, 0], part(v, 0, 1)) + dot(u[1, 1], part(v, 1, 1)),
        }

    def lower_across(u, v):
        return {
            (0, 0): dot(u[0, 0], v[0, 0], True),
            (1, 0): dot(u[1, 0], v[0, 0], True),
            (1, 1): dot(u[1, 0], v[1, 0], True) + dot(u[1, 1], v[1, 1], True),
        }

    def change(x, gap):
        phi = blocks(half_precise, blocks(times, gap, half_lower))
        y = lower_lower(phi, x)
        return blocks(minus, y, lower_lower(phi, y))

    gram = acc[:, :k] / 7168
    diagonals = [part(gram, i, i) * one for i in (0, 1)]
    down = lax.rsqrt(jnp.concatenate([jnp.sum(d, axis=1, keepdims=True) for d in diagonals], axis=0))
    across = lax.rsqrt(jnp.concatenate([jnp.sum(d, axis=0, keepdims=True) for d in diagonals], axis=1))
    a = gram * down * across
    high, low = halves(a)
    phi = {at: (part(a, *at) - eye[at]) * half_lower[at] for at in spots}
    x = blocks(half_precise, blocks(minus, eye, blocks(minus, phi, lower_lower(phi, phi))))
    gap = blocks(minus, lower_across(lower_whole(x, high), x), eye)
    x = blocks(half_precise, blocks(lambda u, v: u.astype(F32) - v, x, change(x, gap)))
    both = blocks(halves, blocks(lambda u, v: u + v, lower_whole(x, high), lower_whole(x, low)))
    left, rest = (blocks(lambda u: u[i], both) for i in (0, 1))
    gap = blocks(lambda u, v, w: u + v - w, lower_across(left, x), lower_across(rest, x), eye)
    gap_ref[0, 0] = sum(jnp.sum(gap[at] * gap[at] * (2.0 * half_lower[at])) for at in spots)
    x = blocks(lambda u, v: u.astype(F32) - v, x, change(x, gap))
    x_ref[:h, h:] = jnp.zeros((h, h), F32)
    for i, j in spots:
        x_ref[i * h:(i + 1) * h, j * h:(j + 1) * h] = x[i, j] * across[:, j * h:(j + 1) * h]


def finish_kernel(x_ref, m_ref, rows_ref, basis_ref, c_ref):
    h = x_ref.shape[0] // 2
    rows = jnp.concatenate([rows_ref[0], rows_ref[1]], axis=1)
    m, m_low = halves(m_ref[...])
    for at, width in ((0, h), (h, 2 * h)):
        high, low = halves(x_ref[at:at + h, :width])
        c_ref[at:at + h] = (dot(high, m[:width]) + (dot(high, m_low[:width]) + dot(low, m[:width]))).astype(BF16)
        basis_ref[:, at:at + h] = dot(rows[:, :width], high, True) + dot(rows[:, :width], low, True)


def local(gate_weights, test_blocks):
    weights = gate_weights.reshape(SIDE, SIDE, 2, 2, CHIP_ROWS, 512)
    n = len(ORDERS) // 2
    slot = lambda step, kind, *lead: pltpu.VMEM((2 * n, *lead, *(SIDE for _ in range(3 - step)), ROWS, LANES), kind)
    turning = pltpu.VMEM((2 * n, SIDE, SIDE, 2, ROWS, 512), BF16)
    scratch = [
        pltpu.VMEM((512, 512), BF16),
        pltpu.VMEM((512, 1024), F32),
        pltpu.VMEM((n, SIDE, SIDE, 2, 2, ROWS, 512), BF16),
        pltpu.VMEM((2, 2 * n, SIDE, SIDE, SIDE, ROWS, LANES), BF16),
        turning, turning, slot(0, BF16), slot(0, BF16),
        slot(1, BF16, 3), slot(1, F32), slot(2, F32, 3), slot(2, F32), slot(3, F32, 3),
        pltpu.SemaphoreType.DMA((2,)),
        pltpu.SemaphoreType.DMA((6 * n,)),
    ]
    for size in (18, 1, 20, 20, 8):
        scratch += [pltpu.SemaphoreType.DMA((size * n,))] * 2
    vmem, smem, hbm = (pl.BlockSpec(memory_space=m) for m in (pltpu.VMEM, pltpu.SMEM, pl.ANY))
    x, gap, acc, rows = pl.pallas_call(
        sum_kernel,
        out_shape=(
            jax.ShapeDtypeStruct((512, 512), F32),
            jax.ShapeDtypeStruct((1, 1), F32),
            jax.ShapeDtypeStruct((512, 1024), F32),
            jax.ShapeDtypeStruct((2, 224, HALF), BF16),
        ),
        in_specs=[hbm, hbm],
        out_specs=(vmem, smem, hbm, vmem),
        scratch_shapes=scratch,
        compiler_params=pltpu.CompilerParams(collective_id=0, has_side_effects=True, vmem_limit_bytes=VMEM_LIMIT),
    )(weights, test_blocks[0])

    def quick():
        return pl.pallas_call(
            finish_kernel,
            grid=(1,),
            out_shape=(jax.ShapeDtypeStruct((224, 512), F32), jax.ShapeDtypeStruct((512, 512), BF16)),
            in_specs=[
                pl.BlockSpec((512, 512), lambda i: (0, 0)),
                pl.BlockSpec((512, 512), lambda i: (0, 1)),
                pl.BlockSpec((2, 224, HALF), lambda i: (0, 0, 0)),
            ],
            out_specs=(pl.BlockSpec((224, 512), lambda i: (0, 0)), pl.BlockSpec((512, 512), lambda i: (0, 0))),
            compiler_params=pltpu.CompilerParams(vmem_limit_bytes=32 << 20),
        )(x, acc, rows)

    def exact():
        lower = jnp.linalg.cholesky(acc[:, :512] / 7168)
        x = lax.linalg.triangular_solve(lower, jnp.eye(512, dtype=F32), left_side=True, lower=True)
        high = functools.partial(jnp.dot, precision=lax.Precision.HIGHEST)
        s = jnp.concatenate([rows[0], rows[1]], axis=1).astype(F32)
        return high(s, x.T), high(x, acc[:, 512:]).astype(BF16)

    basis, coefficients = lax.cond(gap[0, 0] < 0.1, quick, exact)
    return basis, coefficients[None]


def solution(mesh):
    placed = (P(None, "expert", "tensor"), P("expert", "tensor", None))
    return jax.shard_map(
        local,
        mesh=mesh,
        in_specs=placed,
        out_specs=(P("expert", None), P("expert", None, "tensor")),
        check_vma=False,
    )
```

```python
import functools

import jax
import jax.numpy as jnp
from jax import lax
from jax.experimental import pallas as pl
from jax.experimental.pallas import tpu as pltpu
from jax.sharding import PartitionSpec as P

MESH = pl.DeviceIdType.MESH
F32, BF16 = jnp.float32, jnp.bfloat16
SIDE = 4
CHIP_ROWS = 112
HALF = 256
LANES = 128
VMEM_LIMIT = 62 << 20
ROWS = 16
ORDERS = ("xzy", "xyz", "yxz", "yzx", "xyz", "yxz", "zxy", "xyz", "zxy", "zyx", "zxy", "yxz", "zyx", "yxz")
AROUND = (2, 3, 7, 8, 11, 12, 13)
PASSED = (0, 1, 4, 5, 6, 10)
TURN_ORDERS = ("xyz", "yzx", "zxy")
PLAN = (
    ("turn", 0, 0), ("turn", 1, 0), ("turn", 2, 0), ("turn", 3, 0), ("turn", 4, 0), ("turn", 5, 0), ("turn", 6, 0),
    ("turn", 7, 0), ("turn", 8, 0), ("turn", 9, 0), ("turn", 10, 0), ("turn", 11, 0), ("turn", 12, 0), ("turn", 13, 0),
    ("turn", 1, 1), ("turn", 2, 1), ("turn", 0, 1), ("turn", 4, 1), ("turn", 5, 1), ("turn", 3, 1), ("turn", 7, 1),
    ("turn", 8, 1), ("turn", 6, 1), ("turn", 10, 1), ("turn", 11, 1), ("turn", 9, 1), ("turn", 13, 1), ("turn", 1, 2),
    ("turn", 12, 1), ("turn", 0, 2), ("turn", 4, 2), ("turn", 2, 2), ("turn", 3, 2), ("turn", 7, 2), ("turn", 5, 2),
    ("turn", 6, 2), ("turn", 10, 2), ("turn", 8, 2), ("turn", 9, 2), ("turn", 13, 2), ("turn", 11, 2), ("pair", 0),
    ("turn", 12, 2), ("both", 0), ("pair", 1), ("both", 1), ("pair", 2), ("pair", 3), ("both", 2), ("both", 3),
    ("pair", 4), ("both", 4), ("pair", 5), ("pair", 6), ("onward", 2), ("onward", 3), ("add", 0, 0), ("both", 5),
    ("both", 6), ("add", 5, 0), ("add", 6, 0), ("onward", 8), ("add", 1, 0), ("add", 2, 0), ("add", 9, 0),
    ("add", 3, 0), ("add", 0, 1), ("add", 4, 0), ("onward", 11), ("onward", 7), ("onward", 13), ("add", 5, 1),
    ("add", 1, 1), ("add", 10, 0), ("onward", 12), ("add", 6, 1), ("add", 9, 1), ("add", 0, 2), ("add", 8, 0),
    ("add", 2, 1), ("add", 4, 1), ("add", 3, 1), ("add", 5, 2), ("add", 7, 0), ("add", 1, 2), ("add", 11, 0),
    ("add", 10, 1), ("add", 12, 0), ("add", 9, 2), ("add", 13, 0), ("add", 2, 2), ("add", 6, 2), ("further", 0, 1),
    ("add", 4, 2), ("further", 5, 1), ("add", 8, 1), ("further", 1, 1), ("add", 3, 2), ("add", 7, 1), ("add", 10, 2),
    ("add", 11, 1), ("further", 9, 1), ("further", 2, 1), ("further", 0, 0), ("further", 4, 1), ("add", 12, 1),
    ("further", 6, 1), ("add", 13, 1), ("add", 8, 2), ("further", 5, 0), ("further", 3, 1), ("further", 1, 0),
    ("add", 7, 2), ("further", 10, 1), ("add", 11, 2), ("further", 9, 0), ("further", 2, 0), ("further", 4, 0),
    ("further", 8, 1), ("add", 13, 2), ("forward", 0), ("add", 12, 2), ("further", 3, 0), ("further", 7, 1),
    ("further", 11, 1), ("further", 6, 0), ("forward", 5), ("forward", 1), ("further", 10, 0), ("share_rest", 9),
    ("further", 13, 1), ("share_rest", 2), ("forward", 4), ("further", 8, 0), ("forward", 6), ("share_rest", 0),
    ("further", 12, 1), ("further", 11, 0), ("share_rest", 3), ("forward", 10), ("share_rest", 1), ("further", 7, 0),
    ("further", 13, 0), ("share_rest", 5), ("share_rest", 4), ("multiply", 0), ("further", 12, 0), ("multiply", 1),
    ("share_rest", 8), ("share_rest", 6), ("multiply", 2), ("share_rest", 10), ("share_rest", 11), ("multiply", 4),
    ("share_rest", 7), ("multiply", 5), ("share_rest", 13), ("share_rest", 12), ("multiply", 3), ("multiply", 6),
)


def where():
    t, e = lax.axis_index("tensor"), lax.axis_index("expert")
    return {"y": e // 8, "x": (e // 2) % 4, "z": (e % 2) * 2 + t // 2, "c": t % 2}


def device(at):
    return (at["z"] % 2) * 2 + at["c"], (at["y"] * 4 + at["x"]) * 2 + at["z"] // 2


def moved(at, axis, by):
    return {**at, axis: lax.rem(at[axis] + by, 2 if axis == "c" else SIDE)}


def send(src, dst, sems, index, at):
    copy = pltpu.make_async_remote_copy(
        src_ref=src, dst_ref=dst, send_sem=sems[0].at[index], recv_sem=sems[1].at[index],
        device_id=device(at), device_id_type=MESH,
    )
    copy.start()
    return copy


def cut(ref, fixed, rows=None, lead=(), dims="yxz", extra=()):
    tail = () if rows is None else (*extra, rows)
    return ref.at[(*lead, *(fixed.get(d, slice(None)) for d in dims), *tail)]


def sum_kernel(g_hbm, t_hbm, x_ref, gap_ref, acc_hbm, rows_ref, t_ref, acc, g, f_ref, turned1, turned2, landed, q,
               stage1, sums1, stage2, sums2, stage3, own_sem, local_sem, *sems):
    turn_sems, core_sems, rs_sems, ag_sems, pair_sems = (sems[2 * i:2 * i + 2] for i in range(5))
    load = pltpu.make_async_copy(t_hbm, t_ref, own_sem.at[0])
    load.start()
    me = where()
    c = me["c"]
    twin = moved(me, "c", 1)
    peers = [twin] + [moved(me, a, k) for a in "xyz" for k in (1, 2, 3)]
    barrier = pltpu.get_barrier_semaphore()
    for peer in peers:
        pl.semaphore_signal(barrier, inc=1, device_id=device(peer), device_id_type=MESH)
    pl.semaphore_wait(barrier, len(peers))
    sent = []

    def part_rows(p):
        return pl.ds(p * ROWS, ROWS)

    def received(copies):
        for copy in copies:
            copy.wait_recv()

    turning, moves = {}, {}

    def turned(unit, step):
        kept, started = turning.pop((unit, step), (None, ()))
        if kept is not None:
            kept.wait()
        received(started)

    def turn(unit, step):
        axis, p, lo = TURN_ORDERS[unit % 3][step], unit // 2, unit % 2
        if step:
            turned(unit, step - 1)
        place = lambda spot: {axis: spot[axis] // 2 if axis == "z" else spot[axis]}
        between = lambda ref, fixed: cut(ref, fixed, lead=(unit,))
        first = lambda fixed: cut(g_hbm, fixed, part_rows(p), extra=(lo,))
        last = lambda fixed: cut(g, fixed, lead=(p,), extra=(lo,), rows=slice(None))
        source = lambda fixed: between((turned1, turned2)[step - 1], fixed) if step else first(fixed)
        target = lambda fixed: last(fixed) if step == 2 else between((turned1, turned2)[step], fixed)
        kept = pltpu.make_async_copy(source(place(me)), target(place(me)), local_sem.at[unit * 3 + step])
        kept.start()
        started = []
        for k in (2,) if axis == "z" else (2, 1, 3):
            peer = moved(me, axis, k)
            index = unit * 9 + step * 3 + k - 1
            started.append(send(source(place(peer)), target(place(me)), turn_sems, index, peer))
        sent.extend(started)
        turning[unit, step] = kept, started

    def product(p, y, column):
        left = g[p, y].reshape(16 * ROWS, 512)
        right = t_ref[:, pl.ds(pl.multiple_of(column * HALF, HALF), HALF)]
        return jnp.dot(left, right, preferred_element_type=F32).reshape(SIDE, SIDE, ROWS, HALF)

    pairs, shares = {}, {}

    def pair(p):
        turned(2 * p, 2)
        turned(2 * p + 1, 2)

        @pl.loop(0, SIDE)
        def _(y):
            value = product(p, y, 1 - c).astype(BF16)
            for h in (0, 1):
                q[2 * p + h, y] = value[..., h * LANES:(h + 1) * LANES]

        units = pl.ds(2 * p, 2)
        pairs[p] = send(q.at[units], landed.at[units], core_sems, p, twin)

    def both(p):
        pairs[p].wait_send()
        pairs[p].wait_recv()

        @pl.loop(0, SIDE)
        def _(y):
            value = product(p, y, c)
            for h in (0, 1):
                unit = 2 * p + h
                part = value[..., h * LANES:(h + 1) * LANES]
                q[unit, y] = (part + landed[unit, y].astype(F32)).astype(BF16)

        for unit in (2 * p, 2 * p + 1):
            if unit in AROUND:
                around(unit)
            else:
                scatter(unit, 0)

    sources, slots, totals = (q, sums1, sums2), (stage1, stage2, stage3), (sums1, sums2)

    def left_after(p, step):
        return "".join(d for d in "yxz" if d not in ORDERS[p][:step])

    def scatter(p, step):
        axis, moves[p] = ORDERS[p][step], []
        for k in (2, 1, 3):
            peer = moved(me, axis, k)
            source = cut(sources[step], {axis: peer[axis]}, lead=(p,), dims=left_after(p, step))
            moves[p].append(send(source, slots[step].at[p, k - 1], rs_sems, p * 10 + step * 3 + k - 1, peer))
        sent.extend(moves[p])

    def halfway(p, at, half):
        axis, across, _ = ORDERS[p][0], *left_after(p, 1)
        return cut(q, {axis: at[axis], across: pl.ds(2 * half, 2)}, lead=(p,))

    def around(p):
        axis = ORDERS[p][0]
        moves[p] = [
            send(halfway(p, moved(me, axis, 2), half), stage1.at[p, 1, pl.ds(2 * half, 2)], rs_sems,
                 p * 10 + (1, 9)[half], moved(me, axis, k))
            for half, k in enumerate((1, 3))
        ]
        sent.extend(moves[p])

    def onward(p):
        axis, passed, moves[p] = ORDERS[p][0], moves[p], []
        for half, k in enumerate((1, 3)):
            passed[half].wait_recv()
            peer = moved(me, axis, k)
            mine = halfway(p, peer, half)
            for i in (0, 1):
                mine[i] = (mine[i].astype(F32) + stage1[p, 1, 2 * half + i].astype(F32)).astype(BF16)
            source = cut(q, {axis: peer[axis]}, lead=(p,))
            moves[p].append(send(source, stage1.at[p, k - 1], rs_sems, p * 10 + k - 1, peer))
        sent.extend(moves[p])

    def add(p, step):
        axis = ORDERS[p][step]
        ways = (0, 2) if step == 0 and p in AROUND else (0, 1, 2)
        received(moves[p])
        mine = cut(sources[step], {axis: me[axis]}, lead=(p,), dims=left_after(p, step))

        def total(at):
            value = mine[(*at,)].astype(F32)
            for k in ways:
                value += slots[step][(p, k, *at)].astype(F32)
            return value

        if step == 0:
            @pl.loop(0, SIDE)
            def _(a):
                totals[0][p, a] = total((a,))
        elif step == 1:
            totals[1][p] = total((slice(None),))
        else:
            f_ref[c, p, me["y"], me["x"], me["z"]] = total((slice(None),)).astype(BF16)
        if step < 2:
            scatter(p, step + 1)
        else:
            gather(p, 2)

    def gather(p, step):
        part = cut(f_ref, {a: me[a] for a in ORDERS[p][:step + 1]}, lead=(c, p))
        ways = (1, 3) if step == 0 and p in PASSED else (2, 1, 3)
        moves[p] = [
            send(part, part, ag_sems, p * 10 + step * 3 + k - 1, moved(me, ORDERS[p][step], k)) for k in ways
        ]
        sent.extend(moves[p])

    def further(p, step):
        received(moves[p])
        gather(p, step)
        if step == 0:
            shares[p] = []
            share(p, 0)

    def piece(p, k, half=None):
        axis, across, _ = ORDERS[p][0], *left_after(p, 1)
        fixed = {axis: lax.rem(me[axis] + SIDE - k, SIDE)}
        if half is not None:
            fixed[across] = pl.ds(2 * half, 2)
        return cut(f_ref, fixed, lead=(c, p))

    def share(p, k):
        shares[p].append(send(piece(p, k), piece(p, k), pair_sems, p * SIDE + k, twin))
        sent.append(shares[p][-1])

    def forward(p):
        came, moves[p] = moves[p], []
        for half, k in enumerate((1, 3)):
            came[half].wait_recv()
            part = piece(p, k, half)
            moves[p].append(send(part, part, ag_sems, p * 10 + (1, 9)[half], moved(me, ORDERS[p][0], k)))
            share(p, k)
        sent.extend(moves[p])

    def share_rest(p):
        for copy, k in zip(moves[p], (2, 2) if p in PASSED else (2, 1, 3)):
            copy.wait_recv()
            if p not in PASSED:
                share(p, k)
        if p in PASSED:
            share(p, 2)

    def multiply(p):
        units = (2 * p, 2 * p + 1)
        for unit in units:
            received(shares[unit])
        s = jnp.concatenate([f_ref[h, unit].reshape(64 * ROWS, LANES) for h in (0, 1) for unit in units], axis=1)
        w = g[p].reshape(64 * ROWS, 512)
        contract = functools.partial(
            lax.dot_general, dimension_numbers=(((0,), (0,)), ((), ())), preferred_element_type=F32
        )
        top = contract(s[:, :HALF], jnp.concatenate([s[:, :HALF], w], axis=1))
        acc[:HALF, :HALF] += top[:, :HALF]
        acc[:HALF, 2 * HALF:] += top[:, HALF:]
        acc[HALF:] += contract(s[:, HALF:], jnp.concatenate([s, w], axis=1))

    acc[...] = jnp.zeros_like(acc)
    load.wait()
    steps = {f.__name__: f for f in (turn, pair, both, onward, add, further, forward, share_rest, multiply)}
    for name, *args in PLAN:
        steps[name](*args)

    for core in (0, 1):
        for lo in (0, 1):
            for unit in range(len(ORDERS)):
                at, lanes = pl.ds(lo * CHIP_ROWS + unit // 2 * ROWS, ROWS), pl.ds(unit % 2 * LANES, LANES)
                rows_ref[core, at, lanes] = f_ref[core, unit, me["y"], me["x"], me["z"] // 2 * 2 + lo]
    store = pltpu.make_async_copy(acc, acc_hbm, own_sem.at[1])
    store.start()
    factor(acc, x_ref, gap_ref)
    store.wait()
    for copy in sent:
        copy.wait_send()


def dot(u, v, across=False):
    return lax.dot_general(
        u.astype(BF16), v.astype(BF16), (((1,), (1 if across else 0,)), ((), ())), preferred_element_type=F32
    )


def halves(u):
    high = u.astype(BF16)
    return high, (u - high.astype(F32)).astype(BF16)


def factor(acc, x_ref, gap_ref):
    k = acc.shape[0]
    h = k // 2
    spots = ((0, 0), (1, 0), (1, 1))
    part = lambda u, i, j: u[i * h:(i + 1) * h, j * h:(j + 1) * h]
    blocks = lambda f, *us: {at: f(*(u[at] for u in us)) for at in spots}
    row = lax.broadcasted_iota(jnp.int32, (h, h), 0)
    col = lax.broadcasted_iota(jnp.int32, (h, h), 1)
    one = (row == col).astype(F32)
    half = jnp.where(row > col, 1.0, 0.5 * one)
    eye = {(0, 0): one, (1, 0): jnp.zeros_like(one), (1, 1): one}
    half_lower = {(0, 0): half, (1, 0): jnp.ones_like(one), (1, 1): half}
    minus = lambda u, v: u - v
    times = lambda u, v: u * v
    half_precise = lambda u: u.astype(BF16)

    def lower_lower(u, v):
        return {
            (0, 0): dot(u[0, 0], v[0, 0]),
            (1, 0): dot(u[1, 0], v[0, 0]) + dot(u[1, 1], v[1, 0]),
            (1, 1): dot(u[1, 1], v[1, 1]),
        }

    def lower_symmetric(u, v):
        return {
            (0, 0): dot(u[0, 0], part(v, 0, 0)),
            (1, 0): dot(u[1, 0], part(v, 0, 0)) + dot(u[1, 1], part(v, 1, 0)),
            (1, 1): dot(u[1, 0], part(v, 1, 0), True) + dot(u[1, 1], part(v, 1, 1)),
        }

    def lower_across(u, v):
        return {
            (0, 0): dot(u[0, 0], v[0, 0], True),
            (1, 0): dot(u[1, 0], v[0, 0], True),
            (1, 1): dot(u[1, 0], v[1, 0], True) + dot(u[1, 1], v[1, 1], True),
        }

    def change(x, gap):
        phi = blocks(half_precise, blocks(times, gap, half_lower))
        y = lower_lower(phi, x)
        return blocks(minus, y, lower_lower(phi, y))

    gram = acc[:, :k] / 7168
    diagonals = [part(gram, i, i) * one for i in (0, 1)]
    down = lax.rsqrt(jnp.concatenate([jnp.sum(d, axis=1, keepdims=True) for d in diagonals], axis=0))
    across = lax.rsqrt(jnp.concatenate([jnp.sum(d, axis=0, keepdims=True) for d in diagonals], axis=1))
    a = gram * down * across
    high, low = halves(a)
    phi = {at: (part(a, *at) - eye[at]) * half_lower[at] for at in spots}
    x = blocks(half_precise, blocks(minus, eye, blocks(minus, phi, lower_lower(phi, phi))))
    gap = blocks(minus, lower_across(lower_symmetric(x, high), x), eye)
    x = blocks(half_precise, blocks(lambda u, v: u.astype(F32) - v, x, change(x, gap)))
    both = blocks(halves, blocks(lambda u, v: u + v, lower_symmetric(x, high), lower_symmetric(x, low)))
    left, rest = (blocks(lambda u: u[i], both) for i in (0, 1))
    gap = blocks(lambda u, v, w: u + v - w, lower_across(left, x), lower_across(rest, x), eye)
    gap_ref[0, 0] = sum(jnp.sum(gap[at] * gap[at] * (2.0 * half_lower[at])) for at in spots)
    x = blocks(lambda u, v: u.astype(F32) - v, x, change(x, gap))
    x_ref[:h, h:] = jnp.zeros((h, h), F32)
    for i, j in spots:
        x_ref[i * h:(i + 1) * h, j * h:(j + 1) * h] = x[i, j] * across[:, j * h:(j + 1) * h]


def finish_kernel(x_ref, m_ref, rows_ref, basis_ref, c_ref):
    h = x_ref.shape[0] // 2
    rows = jnp.concatenate([rows_ref[0], rows_ref[1]], axis=1)
    m, m_low = halves(m_ref[...])
    for at, width in ((0, h), (h, 2 * h)):
        high, low = halves(x_ref[at:at + h, :width])
        c_ref[at:at + h] = (dot(high, m[:width]) + (dot(high, m_low[:width]) + dot(low, m[:width]))).astype(BF16)
        basis_ref[:, at:at + h] = dot(rows[:, :width], high, True) + dot(rows[:, :width], low, True)


def local(gate_weights, test_blocks):
    weights = gate_weights.reshape(SIDE, SIDE, 2, 2, CHIP_ROWS, 512)
    n = len(ORDERS) // 2
    slot = lambda step, kind, *lead: pltpu.VMEM((2 * n, *lead, *(SIDE for _ in range(3 - step)), ROWS, LANES), kind)
    turning = pltpu.VMEM((2 * n, SIDE, SIDE, 2, ROWS, 512), BF16)
    scratch = [
        pltpu.VMEM((512, 512), BF16),
        pltpu.VMEM((512, 1024), F32),
        pltpu.VMEM((n, SIDE, SIDE, 2, 2, ROWS, 512), BF16),
        pltpu.VMEM((2, 2 * n, SIDE, SIDE, SIDE, ROWS, LANES), BF16),
        turning, turning, slot(0, BF16), slot(0, BF16),
        slot(1, BF16, 3), slot(1, F32), slot(2, F32, 3), slot(2, F32), slot(3, F32, 3),
        pltpu.SemaphoreType.DMA((2,)),
        pltpu.SemaphoreType.DMA((6 * n,)),
    ]
    for size in (18, 1, 20, 20, 8):
        scratch += [pltpu.SemaphoreType.DMA((size * n,))] * 2
    vmem, smem, hbm = (pl.BlockSpec(memory_space=m) for m in (pltpu.VMEM, pltpu.SMEM, pl.ANY))
    x, gap, acc, rows = pl.pallas_call(
        sum_kernel,
        out_shape=(
            jax.ShapeDtypeStruct((512, 512), F32),
            jax.ShapeDtypeStruct((1, 1), F32),
            jax.ShapeDtypeStruct((512, 1024), F32),
            jax.ShapeDtypeStruct((2, 224, HALF), BF16),
        ),
        in_specs=[hbm, hbm],
        out_specs=(vmem, smem, hbm, vmem),
        scratch_shapes=scratch,
        compiler_params=pltpu.CompilerParams(collective_id=0, has_side_effects=True, vmem_limit_bytes=VMEM_LIMIT),
    )(weights, test_blocks[0])

    def quick():
        return pl.pallas_call(
            finish_kernel,
            grid=(1,),
            out_shape=(jax.ShapeDtypeStruct((224, 512), F32), jax.ShapeDtypeStruct((512, 512), BF16)),
            in_specs=[
                pl.BlockSpec((512, 512), lambda i: (0, 0)),
                pl.BlockSpec((512, 512), lambda i: (0, 1)),
                pl.BlockSpec((2, 224, HALF), lambda i: (0, 0, 0)),
            ],
            out_specs=(pl.BlockSpec((224, 512), lambda i: (0, 0)), pl.BlockSpec((512, 512), lambda i: (0, 0))),
            compiler_params=pltpu.CompilerParams(vmem_limit_bytes=32 << 20),
        )(x, acc, rows)

    def exact():
        lower = jnp.linalg.cholesky(acc[:, :512] / 7168, symmetrize_input=False)
        x = lax.linalg.triangular_solve(lower, jnp.eye(512, dtype=F32), left_side=True, lower=True)
        high = functools.partial(jnp.dot, precision=lax.Precision.HIGHEST)
        s = jnp.concatenate([rows[0], rows[1]], axis=1).astype(F32)
        return high(s, x.T), high(x, acc[:, 512:]).astype(BF16)

    basis, coefficients = lax.cond(gap[0, 0] < 0.1, quick, exact)
    return basis, coefficients[None]


def solution(mesh):
    placed = (P(None, "expert", "tensor"), P("expert", "tensor", None))
    return jax.shard_map(
        local,
        mesh=mesh,
        in_specs=placed,
        out_specs=(P("expert", None), P("expert", None, "tensor")),
        check_vma=False,
    )
```
